32 devices in a mesh: group: 4 (over z), dom: 8 (over y, x, core).
Axes of the slice: x: 2, y: 2, z: 4, core: 2. Of those that a mesh axis runs over, the one named last changes fastest.
Arguments:
- feats: bfloat16 [4096, 1024], P(('group', 'dom')), may hold values from -6 to 6
- history: bfloat16 [4096, 1024], P(('group', 'dom')), may hold values from -0.25 to 2
- grad_out: bfloat16 [4096, 1024], P(('group', 'dom')), may hold values from -6 to 6
- w_first: bfloat16 [1024, 1024], replicated, may hold values from -0.1875 to 0.1875
- w_second: bfloat16 [1024, 1024], replicated, may hold values from -0.1875 to 0.1875
- send_index: int32 [32, 8, 16], P(('group', 'dom')), may hold values from 0 to 127, as said below
- halo_index: int32 [16384], P(('group', 'dom')), may hold values from 0 to 127
- hub_rows: int32 [32, 32], P(('group', 'dom')), may hold values from 0 to 127
- tile_cols: int32 [32, 4], P(('group', 'dom')), may hold values from 0 to 5
- tile_vals: bfloat16 [32, 4, 128, 128], P(('group', 'dom')), may hold values from -0.25 to 0.25
Outputs:
- new_history: bfloat16 [4096, 1024], P(('group', 'dom'))
- embed_grad: bfloat16 [4096, 1024], P(('group', 'dom'))
- grad_first: float32 [1024, 1024], P(('group', 'dom'))
- grad_second: float32 [1024, 1024], P(('group', 'dom'))
The draws below stay inside these ranges and needn't reach their ends.
Inputs may be any that keep to these rules, and one draw needn't show every extreme that they name: `send_index`: for each device and each dom peer the 16 rows are distinct. `halo_index`: A value q names slot q % 16 of the rows received from dom peer q // 16 of the same group; values may repeat. `hub_rows`: rows may repeat. `tile_cols`: source tile 0 is the device's own rows, tiles 1 to 4 are halo tiles, tiles 5 and 6 are hub tiles; values may repeat in a row.
All inputs are finite; a program needn't handle non-finite values.
Results may differ from the reference program's by a relative error of at most 0.006.
Values may be sent and summed in bfloat16 or wider, within the bound.
A program may use at most 64 MiB of HBM per device.

```python
import math
import jax
import jax.numpy as jnp
import numpy as np
from jax import lax

D = 1024
V_DEV = 128
TILE = 128
TPR = 4
CAP = 16
HALO = 512
HUB_DEV = 32
VERTS = 4096
RT_DEV = 1
RTILES = 32
SLOTS = 128
SRC = 768
ST = 6
N_GROUP = 4
N_DOM = 8
DEVICES = 32


def draw_send_index(key, part):
    scores = jax.random.randint(key, (DEVICES, N_DOM, V_DEV), 0, 2 ** 16)
    scores = scores * V_DEV + jnp.arange(V_DEV, dtype=jnp.int32)[None, None, :]
    ranking = jnp.argsort(scores, axis=-1, stable=True)
    return ranking[:, :, :CAP].astype(jnp.int32)


def place_ends(array, stream_key, low, top_value):
    extent = array.shape
    index_at = [jax.random.randint(jax.random.fold_in(stream_key, axis), (), 0, extent[axis]) for axis in range(len(extent))]
    array = array.at[tuple(index_at)].set(low)
    longest = extent.index(max(extent))
    index_at[longest] = (index_at[longest] + 1) % extent[longest]
    return array.at[tuple(index_at)].set(top_value)


def spiked(drawn, key, source, target, blocks, factor):
    owner, partner = [(jnp.arange(drawn.shape[dim]) // (drawn.shape[dim] // blocks)).reshape([-1 if axis == dim else 1 for axis in range(drawn.ndim)]) for dim in (source, target)]
    chosen = jax.random.permutation(key, blocks)[partner]
    strong = (owner == chosen) | (owner == (partner + blocks // 2) % blocks)
    return jnp.where(strong, factor * drawn, drawn)


def level_of(own_key, dims, split, smallest, top_value):
    def one(dim, parts):
        steps = jax.random.uniform(jax.random.fold_in(jax.random.fold_in(own_key, 6), dim), (parts,), jnp.float32, smallest / len(split), top_value / len(split))
        return jnp.repeat(jnp.exp(steps), dims[dim] // parts).reshape((-1,) + (1,) * (len(dims) - dim - 1))

    loudness = one(*split[0])
    for cut in split[1:]:
        loudness = loudness * one(*cut)
    return loudness


def rank_bounds(amount, slope):
    weights = [(1 << 20) // math.isqrt(grade ** slope) + 1 for grade in range(1, amount + 1)]
    width = 1 + sum(weights) // (1 << 30)
    return np.cumsum(np.array([max(1, weight // width) for weight in weights]))


def ranked_ids(stream_key, shape, amount, lean):
    table = rank_bounds(amount, lean)
    pick = jax.random.randint(jax.random.fold_in(stream_key, 1), shape, 0, int(table[amount - 1]))
    rank = jnp.searchsorted(jnp.asarray(table, jnp.int32), pick, side="right")
    return jax.random.permutation(jax.random.fold_in(stream_key, 2), amount)[rank].astype(jnp.int32)


def centred(own_key, shape, deviation, bound, cuts=(), kind=jnp.bfloat16):
    drawn = jax.random.normal(own_key, shape, jnp.float32) * deviation
    if len(cuts) > 0:
        drawn = level_of(own_key, shape, cuts, -0.22, 0.18) * drawn
    return jnp.clip(drawn, min=-bound, max=bound).astype(kind)


def bell_draw_with(own_key, extent, scale, most, split, heavy, held_as=jnp.bfloat16):
    result = scale * jax.random.normal(own_key, extent, jnp.float32)
    if split:
        result = result * level_of(own_key, extent, split, -0.22, 0.18)
    return jnp.clip(spiked(result, jax.random.fold_in(own_key, 3), *heavy), -most, most).astype(held_as)


def setup_inputs(seed: int = 0) -> dict:
    key_of = jax.random.split(jax.random.key(seed), 11)
    return {
        "feats": centred(key_of[0], (VERTS, D), 1.0, 6.0, ((0, 32),)),
        "history": jnp.clip(-0.25 + 2.25 * jax.random.uniform(key_of[1], (VERTS, D), jnp.float32) ** level_of(key_of[1], (VERTS, D), ((0, 32),), -0.2, 0.2), -0.25, 2.0).astype(jnp.bfloat16),
        "grad_out": bell_draw_with(key_of[2], (VERTS, D), 1.0, 6.0, ((0, 32),), (0, 1, 32, 2.75)),
        "w_first": centred(key_of[3], (D, D), D ** -0.5, 0.1875),
        "w_second": centred(key_of[4], (D, D), D ** -0.5, 0.1875),
        "send_index": draw_send_index(jax.random.fold_in(key_of[10], 71), 0),
        "halo_index": place_ends(ranked_ids(key_of[6], (DEVICES * HALO,), SLOTS, 2), jax.random.fold_in(key_of[6], 3), 0, SLOTS - 1).astype(jnp.int32),
        "hub_rows": place_ends(jax.random.randint(key_of[7], (DEVICES, HUB_DEV), 0, V_DEV), jax.random.fold_in(key_of[7], 1), 0, V_DEV - 1).astype(jnp.int32),
        "tile_cols": place_ends(jax.random.randint(key_of[8], (RTILES, TPR), 0, ST), jax.random.fold_in(key_of[8], 1), 0, ST - 1).astype(jnp.int32),
        "tile_vals": centred(key_of[9], (RTILES, TPR, TILE, TILE), (TPR * TILE) ** -0.5, 0.25, ((0, 32),)),
    }


def source_table(send_index, halo_index, hub_rows):
    blocks = jnp.arange(DEVICES, dtype=jnp.int32)
    dom_of = blocks % N_DOM
    own_rows = blocks[:, None] * V_DEV + jnp.arange(V_DEV, dtype=jnp.int32)[None, :]
    row_base = (jnp.arange(N_GROUP, dtype=jnp.int32)[:, None] * N_DOM + jnp.arange(N_DOM, dtype=jnp.int32)[None, :]) * V_DEV
    sent_rows = send_index.reshape(N_GROUP, N_DOM, N_DOM, CAP) + row_base[:, :, None, None]
    received = jnp.transpose(sent_rows, (0, 2, 1, 3)).reshape(DEVICES, N_DOM * CAP)
    halo_ids = jnp.take_along_axis(received, halo_index.reshape(DEVICES, HALO), axis=1)
    hub_ids = hub_rows.reshape(N_GROUP, N_DOM, HUB_DEV) + row_base[:, :, None]
    hub_panel = jnp.transpose(hub_ids, (1, 0, 2)).reshape(N_DOM, N_GROUP * HUB_DEV)
    hub_all = hub_panel[dom_of]
    return jnp.concatenate([own_rows, halo_ids, hub_all], axis=1).astype(jnp.int32)

def aggregate(table, halo_table, source_ids, tile_cols, tile_vals):
    tile_ids = tile_cols.reshape(DEVICES, RT_DEV, TPR)
    tile_weights = tile_vals.reshape(DEVICES, RT_DEV, TPR, TILE, TILE)
    position = jnp.arange(SRC, dtype=jnp.int32)
    in_halo = (position >= V_DEV) & (position < V_DEV + HALO)

    def per_block(inputs):
        block_ids, block_tiles, block_weights = inputs
        source = jnp.where(in_halo[:, None], halo_table[block_ids], table[block_ids]).reshape(ST, TILE, D)
        picked = source[block_tiles].astype(jnp.float32)
        summed = jnp.einsum('rtij,rtjd->rid', block_weights.astype(jnp.float32), picked, precision=lax.Precision.HIGHEST)
        return summed.reshape(V_DEV, D).astype(jnp.bfloat16)
    return lax.map(per_block, (source_ids, tile_ids, tile_weights)).reshape(VERTS, D)

def spread_back(agg_grad, source_ids, tile_cols, tile_vals):
    tile_ids = tile_cols.reshape(DEVICES, RT_DEV, TPR)
    tile_weights = tile_vals.reshape(DEVICES, RT_DEV, TPR, TILE, TILE)
    kept_rows = jnp.concatenate([jnp.arange(V_DEV, dtype=jnp.int32), jnp.arange(V_DEV + HALO, SRC, dtype=jnp.int32)])

    def per_block(inputs):
        block_tiles, block_weights, grad_rows = inputs
        tile_terms = jnp.einsum('rtij,rid->rtjd', block_weights.astype(jnp.float32), grad_rows.reshape(RT_DEV, TILE, D).astype(jnp.float32), precision=lax.Precision.HIGHEST)
        spread = jnp.zeros((ST, TILE, D), jnp.float32).at[block_tiles].add(tile_terms)
        return spread.reshape(SRC, D)[kept_rows]
    block_grads = lax.map(per_block, (tile_ids, tile_weights, agg_grad.reshape(DEVICES, V_DEV, D)))
    target_ids = source_ids[:, kept_rows]
    return jnp.zeros((VERTS, D), jnp.float32).at[target_ids.reshape(-1)].add(block_grads.reshape(-1, D))

def reference(feats, history, grad_out, w_first, w_second, send_index, halo_index, hub_rows, tile_cols, tile_vals):
    source_ids = source_table(send_index, halo_index, hub_rows)
    agg_first = aggregate(feats, feats, source_ids, tile_cols, tile_vals)
    z_first = jnp.dot(agg_first, w_first, preferred_element_type=jnp.float32)
    new_history = jax.nn.silu(z_first).astype(jnp.bfloat16)
    agg_second = aggregate(new_history, history, source_ids, tile_cols, tile_vals)
    factor = 1.0 / math.sqrt(VERTS)
    grad_second = jnp.dot(grad_out.T, agg_second, preferred_element_type=jnp.float32) * factor
    agg_grad = jnp.dot(grad_out, w_second.T, preferred_element_type=jnp.float32).astype(jnp.bfloat16)
    vertex_grad = spread_back(agg_grad, source_ids, tile_cols, tile_vals)
    gate_value = jax.nn.sigmoid(z_first)
    dz_first = (vertex_grad * gate_value * (1.0 + z_first * (1.0 - gate_value))).astype(jnp.bfloat16)
    grad_first = jnp.dot(dz_first.T, agg_first, preferred_element_type=jnp.float32) * factor
    return (new_history, vertex_grad.astype(jnp.bfloat16), grad_first, grad_second)
```

```python
import math

import jax
import jax.numpy as jnp
from jax import lax
from jax.sharding import PartitionSpec as P

D = 1024
V_DEV = 128
TILE = 128
HALO = 512


def combine_tiles(own_rows, halo_rows, hub_panel, tile_cols, tile_vals):
    source = jnp.concatenate([own_rows, halo_rows, hub_panel], axis=0)
    feature_width = source.shape[1]
    picked = source.reshape(-1, tile_vals.shape[2], feature_width)[tile_cols]
    summed = jnp.einsum("rtij,rtjd->rid", tile_vals, picked, preferred_element_type=jnp.float32)
    return summed.reshape(-1, feature_width).astype(jnp.bfloat16)


def reduce_weight(left_rows, right_rows):
    groups, doms = lax.axis_size("group"), lax.axis_size("dom")
    factor = 1.0 / math.sqrt(left_rows.shape[0] * groups * doms)
    rows = left_rows.shape[0]
    gathered = lax.all_gather(right_rows, "dom", axis=0, tiled=True)
    by_dom = left_rows.reshape(rows, groups, doms, -1).transpose(2, 0, 1, 3).reshape(doms * rows, -1)
    columns = lax.all_to_all(by_dom, "dom", split_axis=0, concat_axis=0, tiled=True)
    product = lax.dot_general(
        columns, gathered, (((0,), (0,)), ((), ())), preferred_element_type=jnp.float32
    )
    summed = lax.psum_scatter(product, "group", scatter_dimension=0, tiled=True)
    return summed * factor


def on_device(
    feats,
    history,
    grad_out,
    w_first,
    w_second,
    send_index,
    halo_index,
    hub_rows,
    tile_cols,
    tile_vals,
):
    routes = send_index[0]
    owned_hubs = hub_rows[0]
    feat_slots = lax.all_to_all(feats[routes], "dom", split_axis=0, concat_axis=0, tiled=True)
    feat_halo = feat_slots.reshape(-1, D)[halo_index]
    hub_first = lax.all_gather(feats[owned_hubs], "group", axis=0, tiled=True)
    agg_first = combine_tiles(feats, feat_halo, hub_first, tile_cols, tile_vals)
    z_first = jnp.dot(agg_first, w_first, preferred_element_type=jnp.float32)
    new_history = jax.nn.silu(z_first).astype(jnp.bfloat16)
    hist_slots = lax.all_to_all(history[routes], "dom", split_axis=0, concat_axis=0, tiled=True)
    hist_halo = hist_slots.reshape(-1, D)[halo_index]
    hub_second = lax.all_gather(new_history[owned_hubs], "group", axis=0, tiled=True)
    agg_second = combine_tiles(new_history, hist_halo, hub_second, tile_cols, tile_vals)
    grad_second = reduce_weight(grad_out, agg_second)
    agg_grad = lax.dot_general(
        grad_out, w_second, (((1,), (1,)), ((), ())), preferred_element_type=jnp.float32
    ).astype(jnp.bfloat16)
    source_tiles = (V_DEV + HALO + hub_second.shape[0]) // TILE
    tile_terms = jnp.einsum(
        "rtij,rid->rtjd",
        tile_vals,
        agg_grad.reshape(-1, TILE, D),
        preferred_element_type=jnp.float32,
    )
    selector = (
        tile_cols[:, :, None] == jnp.arange(source_tiles, dtype=jnp.int32)[None, None, :]
    ).astype(jnp.float32)
    spread = jnp.einsum(
        "rts,rtjd->sjd", selector, tile_terms, precision=lax.Precision.HIGHEST
    ).reshape(-1, D)
    own_grad = spread[:V_DEV]
    hub_grad = lax.psum_scatter(spread[V_DEV + HALO :], "group", scatter_dimension=0, tiled=True)
    vertex_grad = own_grad.at[owned_hubs].add(hub_grad)
    gate_value = jax.nn.sigmoid(z_first)
    dz_first = (vertex_grad * gate_value * (1.0 + z_first * (1.0 - gate_value))).astype(
        jnp.bfloat16
    )
    grad_first = reduce_weight(dz_first, agg_first)
    return (new_history, vertex_grad.astype(jnp.bfloat16), grad_first, grad_second)


def solution(mesh):
    placed = (
        P(("group", "dom"), None),
        P(("group", "dom"), None),
        P(("group", "dom"), None),
        P(),
        P(),
        P(("group", "dom"), None, None),
        P(("group", "dom")),
        P(("group", "dom"), None),
        P(("group", "dom"), None),
        P(("group", "dom"), None, None, None),
    )
    return jax.shard_map(
        on_device,
        mesh=mesh,
        in_specs=placed,
        out_specs=(
            P(("group", "dom"), None),
            P(("group", "dom"), None),
            P(("group", "dom"), None),
            P(("group", "dom"), None),
        ),
        check_vma=False,
    )
```

```python
import functools
import math

import jax
import jax.numpy as jnp
from jax import lax
from jax.experimental import pallas as pl
from jax.experimental.pallas import tpu as pltpu
from jax.sharding import PartitionSpec as P

D = 1024
V_DEV = 128
TILE = 128
HALO = 512


def combine_tiles(own_rows, halo_rows, hub_panel, tile_cols, tile_vals):
    source = jnp.concatenate([own_rows, halo_rows, hub_panel], axis=0)
    feature_width = source.shape[1]
    picked = source.reshape(-1, tile_vals.shape[2], feature_width)[tile_cols]
    summed = jnp.einsum("rtij,rtjd->rid", tile_vals, picked, preferred_element_type=jnp.float32)
    return summed.reshape(-1, feature_width).astype(jnp.bfloat16)


def reduce_weight(left_rows, right_rows):
    groups, doms = lax.axis_size("group"), lax.axis_size("dom")
    factor = 1.0 / math.sqrt(left_rows.shape[0] * groups * doms)
    rows = left_rows.shape[0]
    gathered = lax.all_gather(right_rows, "dom", axis=0, tiled=True)
    by_dom = left_rows.reshape(rows, groups, doms, -1).transpose(2, 0, 1, 3).reshape(doms * rows, -1)
    columns = lax.all_to_all(by_dom, "dom", split_axis=0, concat_axis=0, tiled=True)
    product = lax.dot_general(
        columns, gathered, (((0,), (0,)), ((), ())), preferred_element_type=jnp.float32
    )
    summed = lax.psum_scatter(product, "group", scatter_dimension=0, tiled=True)
    return summed * factor


def on_device(
    feats,
    history,
    grad_out,
    w_first,
    w_second,
    send_index,
    halo_index,
    hub_rows,
    tile_cols,
    tile_vals,
):
    routes = send_index[0]
    owned_hubs = hub_rows[0]
    feat_slots = lax.all_to_all(feats[routes], "dom", split_axis=0, concat_axis=0, tiled=True)
    feat_halo = feat_slots.reshape(-1, D)[halo_index]
    hub_first = lax.all_gather(feats[owned_hubs], "group", axis=0, tiled=True)
    agg_first = combine_tiles(feats, feat_halo, hub_first, tile_cols, tile_vals)
    z_first = jnp.dot(agg_first, w_first, preferred_element_type=jnp.float32)
    new_history = jax.nn.silu(z_first).astype(jnp.bfloat16)
    hist_slots = lax.all_to_all(history[routes], "dom", split_axis=0, concat_axis=0, tiled=True)
    hist_halo = hist_slots.reshape(-1, D)[halo_index]
    hub_second = lax.all_gather(new_history[owned_hubs], "group", axis=0, tiled=True)
    agg_second = combine_tiles(new_history, hist_halo, hub_second, tile_cols, tile_vals)
    grad_second = reduce_weight(grad_out, agg_second)
    agg_grad = lax.dot_general(
        grad_out, w_second, (((1,), (1,)), ((), ())), preferred_element_type=jnp.float32
    ).astype(jnp.bfloat16)
    source_tiles = (V_DEV + HALO + hub_second.shape[0]) // TILE
    tile_terms = jnp.einsum(
        "rtij,rid->rtjd",
        tile_vals,
        agg_grad.reshape(-1, TILE, D),
        preferred_element_type=jnp.float32,
    )
    selector = (
        tile_cols[:, :, None] == jnp.arange(source_tiles, dtype=jnp.int32)[None, None, :]
    ).astype(jnp.float32)
    spread = jnp.einsum(
        "rts,rtjd->sjd", selector, tile_terms, precision=lax.Precision.HIGHEST
    ).reshape(-1, D)
    own_grad = spread[:V_DEV]
    hub_grad = lax.psum_scatter(spread[V_DEV + HALO :], "group", scatter_dimension=0, tiled=True)
    vertex_grad = own_grad.at[owned_hubs].add(hub_grad)
    gate_value = jax.nn.sigmoid(z_first)
    dz_first = (vertex_grad * gate_value * (1.0 + z_first * (1.0 - gate_value))).astype(
        jnp.bfloat16
    )
    grad_first = reduce_weight(dz_first, agg_first)
    return (new_history, vertex_grad.astype(jnp.bfloat16), grad_first, grad_second)


BF16, F32 = jnp.bfloat16, jnp.float32


def dot(left, right, contract=(1, 0)):
    dims = (((contract[0],), (contract[1],)), ((), ()))
    return lax.dot_general(left, right, dims, preferred_element_type=F32)


def halves(weights):
    high = weights.astype(BF16)
    low = (weights - high.astype(F32)).astype(BF16)
    return jnp.concatenate([high, low], axis=0)


def apply_halves(pair, rows):
    both = dot(pair, rows)
    count = pair.shape[0] // 2
    return both[:count] + both[count:]


def window_kernel(
    groups,
    doms,
    feats,
    history,
    grad_out,
    index_rows,
    tile_cols,
    tile_vals,
    w_first,
    w_second,
    new_history,
    embed_grad,
    grad_first,
    grad_second,
    w_first_held,
    w_second_held,
    send_feats,
    send_hist,
    send_hubs,
    send_fresh,
    slots_feats,
    slots_hist,
    hubs_first,
    hubs_second,
    all_grad_out,
    all_agg,
    hub_terms,
    hub_arrived,
    own_grad,
    gate_slope,
    dz_out,
    dz_in,
    agg_out,
    agg_in,
    first_terms,
    first_sent,
    first_in,
    second_terms,
    second_sent,
    second_in,
    rows_out,
    rows_in,
    local_sems,
    send_sems,
    recv_sems,
):
    group, dom = lax.axis_index("group"), lax.axis_index("dom")
    chips = doms // 2
    chip, core = dom // 2, dom % 2
    factor = 1.0 / math.sqrt(V_DEV * groups * doms)
    share = D // (groups * doms)
    dom_peers = [(dom + off) % doms for off in range(1, doms)]
    group_peers = [(group + off) % groups for off in range(1, groups)]
    sibling = dom + 1 - 2 * core
    chip_peers = [((chip + off) % chips) * 2 + core for off in range(1, chips)]
    chip_sources = [((chip + chips - off) % chips) * 2 + core for off in range(1, chips)]
    used = []

    load_second = pltpu.make_async_copy(w_second, w_second_held, local_sems.at[0])
    load_second.start()
    load_first = pltpu.make_async_copy(w_first, w_first_held, local_sems.at[1])
    load_first.start()

    barrier = pltpu.get_barrier_semaphore()
    for peer in dom_peers:
        pl.semaphore_signal(
            barrier, inc=1, device_id=(group, peer), device_id_type=pl.DeviceIdType.MESH
        )
    for peer in group_peers:
        pl.semaphore_signal(
            barrier, inc=1, device_id=(peer, dom), device_id_type=pl.DeviceIdType.MESH
        )

    def send(source, target, to_group, to_dom):
        copy = pltpu.make_async_remote_copy(
            src_ref=source,
            dst_ref=target,
            send_sem=send_sems.at[len(used)],
            recv_sem=recv_sems.at[len(used)],
            device_id=(to_group, to_dom),
            device_id_type=pl.DeviceIdType.MESH,
        )
        used.append(copy)
        copy.start()
        return copy

    def to_doms(source, target):
        return [send(source.at[peer], target.at[dom], group, peer) for peer in dom_peers]

    def to_groups(source, target):
        return [send(source.at[peer], target.at[group], peer, dom) for peer in group_peers]

    def share_to_groups(source, target):
        return [send(source, target.at[group], peer, dom) for peer in group_peers]

    def to_chips(source, target):
        near = send(source, target.at[dom], group, sibling)
        return near, [send(source, target.at[dom], group, peer) for peer in chip_peers]

    def forward(far, target):
        passed = []
        for copy, origin in zip(far, chip_sources):
            copy.wait_recv()
            passed.append(send(target.at[origin], target.at[origin], group, sibling))
        return passed

    def arrived(copies):
        for copy in copies:
            copy.wait_recv()

    sublane = lax.broadcasted_iota(jnp.int32, (V_DEV, V_DEV), 0)
    lane_row = lax.broadcasted_iota(jnp.int32, (1, V_DEV), 1)
    route_cols = (sublane == index_rows[0:1, :]).astype(F32)
    hub_cols = (sublane == index_rows[1:2, :]).astype(F32)
    route_pick = route_cols.T.astype(BF16)
    hub_count = V_DEV // groups
    hub_pick = hub_cols.T[:hub_count].astype(BF16)
    hub_spread = hub_cols.astype(BF16)

    send_feats[...] = dot(route_pick, feats[...]).astype(BF16).reshape(send_feats.shape)
    send_hubs[...] = dot(hub_pick, feats[...]).astype(BF16)
    pl.semaphore_wait(barrier, doms - 1 + groups - 1)
    feat_copies = to_doms(send_feats, slots_feats)
    hub_copies = share_to_groups(send_hubs, hubs_first)
    slots_feats[dom] = send_feats[dom]
    hubs_first[group] = send_hubs[...]
    send_hist[...] = dot(route_pick, history[...]).astype(BF16).reshape(send_hist.shape)
    hist_copies = to_doms(send_hist, slots_hist)
    slots_hist[dom] = send_hist[dom]
    grad_near, grad_far = to_chips(grad_out, all_grad_out)
    all_grad_out[dom] = grad_out[...]

    places = 3 * V_DEV
    place_of = lax.broadcasted_iota(jnp.int32, (places, V_DEV), 0)
    weights = jnp.zeros((V_DEV, places), F32)
    halo_tiles = HALO // TILE
    for tile in range(tile_vals.shape[1]):
        column = tile_cols[0:1, tile : tile + 1]
        target = jnp.where(column == 0, lane_row, lane_row + 2 * V_DEV)
        for halo in range(halo_tiles):
            slot = index_rows[2 + halo : 3 + halo, :] + V_DEV
            target = jnp.where(column == halo + 1, slot, target)
        chosen = (place_of == target).astype(F32).astype(BF16)
        weights = weights + dot(tile_vals[0, tile], chosen, (1, 1))
    own, slot, hub = (weights[:, n * V_DEV : (n + 1) * V_DEV] for n in range(3))
    own_pair, slot_pair, hub_pair = halves(own), halves(slot), halves(hub)

    load_second.wait()
    agg_grad = dot(grad_out[...], w_second_held[...], (1, 1)).astype(BF16)
    hub_terms[...] = apply_halves(halves(hub.T), agg_grad).astype(BF16).reshape(hub_terms.shape)
    term_copies = to_groups(hub_terms, hub_arrived)
    hub_arrived[group] = hub_terms[group]
    own_grad[...] = apply_halves(halves(own.T), agg_grad)

    first = apply_halves(own_pair, feats[...])
    arrived(feat_copies)
    first = first + apply_halves(slot_pair, slots_feats[...].reshape(V_DEV, D))
    arrived(hub_copies)
    first = first + apply_halves(hub_pair, hubs_first[...].reshape(V_DEV, D))
    agg_first = first.astype(BF16)
    all_agg[dom] = agg_first
    agg_near, agg_far = to_chips(all_agg.at[dom], all_agg)

    load_first.wait()
    z_first = dot(agg_first, w_first_held[...])
    gate = 1.0 / (1.0 + jnp.exp(-z_first))
    fresh = (z_first * gate).astype(BF16)
    new_history[...] = fresh
    send_fresh[...] = dot(hub_pick, fresh).astype(BF16)
    fresh_copies = share_to_groups(send_fresh, hubs_second)
    hubs_second[group] = send_fresh[...]
    gate_slope[...] = gate * (1.0 + z_first * (1.0 - gate))

    arrived(term_copies)
    vertex_grad = own_grad[...] + dot(hub_spread, hub_arrived[...].reshape(V_DEV, D))
    embed_grad[...] = vertex_grad.astype(BF16)
    own_grad[...] = vertex_grad * gate_slope[...]
    for g in range(groups):
        for d in range(0, doms * share, TILE):
            start = g * doms * share + d
            block = own_grad[:, start : start + TILE].T.astype(BF16)
            for piece in range(TILE // share):
                dz_out[d // share + piece, g * share : (g + 1) * share, :] = block[
                    piece * share : (piece + 1) * share
                ]
    dz_copies = to_doms(dz_out, dz_in)
    dz_in[dom] = dz_out[dom]

    arrived(hist_copies)
    second = apply_halves(own_pair, new_history[...])
    second = second + apply_halves(slot_pair, slots_hist[...].reshape(V_DEV, D))
    arrived(fresh_copies)
    second = second + apply_halves(hub_pair, hubs_second[...].reshape(V_DEV, D))
    wide = D // doms
    for d in range(doms):
        agg_out[d] = second[:, d * wide : (d + 1) * wide].T.astype(BF16)
    agg_copies = to_doms(agg_out, agg_in)
    agg_in[dom] = agg_out[dom]

    grad_passed = forward(grad_far, all_grad_out)
    agg_passed = forward(agg_far, all_agg)
    arrived([grad_near] + grad_passed)
    arrived(agg_copies)
    total = dot(agg_in[0], all_grad_out[0])
    for d in range(1, doms):
        total = total + dot(agg_in[d], all_grad_out[d])
    per_group = D // groups
    for g in range(groups):
        for n in range(0, per_group, TILE):
            start = g * per_group + n
            block = total[:, start : start + TILE].T
            second_terms[g, n : n + TILE, :] = block
            second_sent[g, n : n + TILE, :] = block.astype(BF16)
    second_copies = to_groups(second_sent, second_in)

    arrived([agg_near] + agg_passed)
    arrived(dz_copies)
    total = dot(dz_in[0], all_agg[0])
    for d in range(1, doms):
        total = total + dot(dz_in[d], all_agg[d])
    first_terms[...] = total.reshape(first_terms.shape)
    first_sent[...] = total.astype(BF16).reshape(first_sent.shape)
    first_copies = to_groups(first_sent, first_in)

    arrived(second_copies)
    second_in[group] = jnp.zeros(second_in.shape[1:], BF16)
    total = second_terms[group]
    for g in range(groups):
        total = total + second_in[g].astype(F32)
    rows_out[...] = (total * factor).reshape(rows_out.shape)
    row_copies = to_doms(rows_out, rows_in)
    rows_in[dom] = rows_out[dom]

    arrived(first_copies)
    first_in[group] = jnp.zeros(first_in.shape[1:], BF16)
    total = first_terms[group]
    for g in range(groups):
        total = total + first_in[g].astype(F32)
    grad_first[...] = total * factor

    arrived(row_copies)
    for d in range(doms):
        grad_second[:, d * wide : (d + 1) * wide] = rows_in[d]
    for copy in used:
        copy.wait_send()


def in_kernel(
    feats, history, grad_out, w_first, w_second, send_index, halo_index, hub_rows, tile_cols, tile_vals
):
    groups, doms = lax.axis_size("group"), lax.axis_size("dom")
    share = D // (groups * doms)
    cap, hubs = send_index.shape[2], hub_rows.shape[1]
    wide, per_group = D // doms, D // groups
    index_rows = jnp.concatenate(
        [
            send_index.reshape(1, V_DEV),
            jnp.tile(hub_rows, (1, groups)),
            halo_index.reshape(HALO // TILE, TILE),
        ],
        axis=0,
    )
    copies = 7 * (doms - 1) + 5 * (groups - 1)
    vmem = pl.BlockSpec(memory_space=pltpu.VMEM)
    hbm = pl.BlockSpec(memory_space=pl.ANY)
    held = pltpu.VMEM
    return pl.pallas_call(
        functools.partial(window_kernel, groups, doms),
        out_shape=(
            jax.ShapeDtypeStruct((V_DEV, D), BF16),
            jax.ShapeDtypeStruct((V_DEV, D), BF16),
            jax.ShapeDtypeStruct((share, D), F32),
            jax.ShapeDtypeStruct((share, D), F32),
        ),
        in_specs=[vmem] * 6 + [hbm] * 2,
        out_specs=(vmem,) * 4,
        scratch_shapes=[
            held((D, D), BF16),
            held((D, D), BF16),
            held((doms, cap, D), BF16),
            held((doms, cap, D), BF16),
            held((hubs, D), BF16),
            held((hubs, D), BF16),
            held((doms, cap, D), BF16),
            held((doms, cap, D), BF16),
            held((groups, hubs, D), BF16),
            held((groups, hubs, D), BF16),
            held((doms, V_DEV, D), BF16),
            held((doms, V_DEV, D), BF16),
            held((groups, hubs, D), BF16),
            held((groups, hubs, D), BF16),
            held((V_DEV, D), F32),
            held((V_DEV, D), F32),
            held((doms, groups * share, V_DEV), BF16),
            held((doms, groups * share, V_DEV), BF16),
            held((doms, wide, V_DEV), BF16),
            held((doms, wide, V_DEV), BF16),
            held((groups, share, D), F32),
            held((groups, share, D), BF16),
            held((groups, share, D), BF16),
            held((groups, per_group, wide), F32),
            held((groups, per_group, wide), BF16),
            held((groups, per_group, wide), BF16),
            held((doms, share, wide), F32),
            held((doms, share, wide), F32),
            pltpu.SemaphoreType.DMA((2,)),
            pltpu.SemaphoreType.DMA((copies,)),
            pltpu.SemaphoreType.DMA((copies,)),
        ],
        compiler_params=pltpu.CompilerParams(
            collective_id=0, has_side_effects=True, vmem_limit_bytes=48 * 1024 * 1024
        ),
    )(feats, history, grad_out, index_rows, tile_cols, tile_vals, w_first, w_second)


def fits_kernel(groups, doms, cap, hubs):
    return (
        D % (groups * doms * 16) == 0
        and TILE % (D // (groups * doms)) == 0
        and D // doms == V_DEV
        and doms * cap == V_DEV
        and groups * hubs == V_DEV
    )


def window(*args):
    send_index, hub_rows = args[5], args[7]
    groups, doms = lax.axis_size("group"), lax.axis_size("dom")
    if fits_kernel(groups, doms, send_index.shape[2], hub_rows.shape[1]):
        return in_kernel(*args)
    return on_device(*args)


def solution(mesh):
    placed = (
        P(("group", "dom"), None),
        P(("group", "dom"), None),
        P(("group", "dom"), None),
        P(),
        P(),
        P(("group", "dom"), None, None),
        P(("group", "dom")),
        P(("group", "dom"), None),
        P(("group", "dom"), None),
        P(("group", "dom"), None, None, None),
    )
    return jax.shard_map(
        window,
        mesh=mesh,
        in_specs=placed,
        out_specs=(
            P(("group", "dom"), None),
            P(("group", "dom"), None),
            P(("group", "dom"), None),
            P(("group", "dom"), None),
        ),
        check_vma=False,
    )
```

```python
import functools
import math

import jax
import jax.numpy as jnp
from jax import lax
from jax.experimental import pallas as pl
from jax.experimental.pallas import tpu as pltpu
from jax.sharding import PartitionSpec as P

D = 1024
V_DEV = 128
TILE = 128
HALO = 512


def combine_tiles(own_rows, halo_rows, hub_panel, tile_cols, tile_vals):
    source = jnp.concatenate([own_rows, halo_rows, hub_panel], axis=0)
    feature_width = source.shape[1]
    picked = source.reshape(-1, tile_vals.shape[2], feature_width)[tile_cols]
    summed = jnp.einsum("rtij,rtjd->rid", tile_vals, picked, preferred_element_type=jnp.float32)
    return summed.reshape(-1, feature_width).astype(jnp.bfloat16)


def reduce_weight(left_rows, right_rows):
    groups, doms = lax.axis_size("group"), lax.axis_size("dom")
    factor = 1.0 / math.sqrt(left_rows.shape[0] * groups * doms)
    rows = left_rows.shape[0]
    gathered = lax.all_gather(right_rows, "dom", axis=0, tiled=True)
    by_dom = left_rows.reshape(rows, groups, doms, -1).transpose(2, 0, 1, 3).reshape(doms * rows, -1)
    columns = lax.all_to_all(by_dom, "dom", split_axis=0, concat_axis=0, tiled=True)
    product = lax.dot_general(
        columns, gathered, (((0,), (0,)), ((), ())), preferred_element_type=jnp.float32
    )
    summed = lax.psum_scatter(product, "group", scatter_dimension=0, tiled=True)
    return summed * factor


def on_device(
    feats,
    history,
    grad_out,
    w_first,
    w_second,
    send_index,
    halo_index,
    hub_rows,
    tile_cols,
    tile_vals,
):
    routes = send_index[0]
    owned_hubs = hub_rows[0]
    feat_slots = lax.all_to_all(feats[routes], "dom", split_axis=0, concat_axis=0, tiled=True)
    feat_halo = feat_slots.reshape(-1, D)[halo_index]
    hub_first = lax.all_gather(feats[owned_hubs], "group", axis=0, tiled=True)
    agg_first = combine_tiles(feats, feat_halo, hub_first, tile_cols, tile_vals)
    z_first = jnp.dot(agg_first, w_first, preferred_element_type=jnp.float32)
    new_history = jax.nn.silu(z_first).astype(jnp.bfloat16)
    hist_slots = lax.all_to_all(history[routes], "dom", split_axis=0, concat_axis=0, tiled=True)
    hist_halo = hist_slots.reshape(-1, D)[halo_index]
    hub_second = lax.all_gather(new_history[owned_hubs], "group", axis=0, tiled=True)
    agg_second = combine_tiles(new_history, hist_halo, hub_second, tile_cols, tile_vals)
    grad_second = reduce_weight(grad_out, agg_second)
    agg_grad = lax.dot_general(
        grad_out, w_second, (((1,), (1,)), ((), ())), preferred_element_type=jnp.float32
    ).astype(jnp.bfloat16)
    source_tiles = (V_DEV + HALO + hub_second.shape[0]) // TILE
    tile_terms = jnp.einsum(
        "rtij,rid->rtjd",
        tile_vals,
        agg_grad.reshape(-1, TILE, D),
        preferred_element_type=jnp.float32,
    )
    selector = (
        tile_cols[:, :, None] == jnp.arange(source_tiles, dtype=jnp.int32)[None, None, :]
    ).astype(jnp.float32)
    spread = jnp.einsum(
        "rts,rtjd->sjd", selector, tile_terms, precision=lax.Precision.HIGHEST
    ).reshape(-1, D)
    own_grad = spread[:V_DEV]
    hub_grad = lax.psum_scatter(spread[V_DEV + HALO :], "group", scatter_dimension=0, tiled=True)
    vertex_grad = own_grad.at[owned_hubs].add(hub_grad)
    gate_value = jax.nn.sigmoid(z_first)
    dz_first = (vertex_grad * gate_value * (1.0 + z_first * (1.0 - gate_value))).astype(
        jnp.bfloat16
    )
    grad_first = reduce_weight(dz_first, agg_first)
    return (new_history, vertex_grad.astype(jnp.bfloat16), grad_first, grad_second)


BF16, F32 = jnp.bfloat16, jnp.float32


def dot(left, right, contract=(1, 0)):
    dims = (((contract[0],), (contract[1],)), ((), ()))
    return lax.dot_general(left, right, dims, preferred_element_type=F32)


def halves(weights):
    high = weights.astype(BF16)
    low = (weights - high.astype(F32)).astype(BF16)
    return jnp.concatenate([high, low], axis=0)


def apply_halves(pair, rows):
    both = dot(pair, rows)
    count = pair.shape[0] // 2
    return both[:count] + both[count:]


def window_kernel(
    groups,
    doms,
    feats_given,
    history_given,
    grad_given,
    w_first,
    w_second,
    send_given,
    halo_given,
    hubs_given,
    cols_given,
    vals_given,
    new_history,
    embed_grad,
    grad_first,
    grad_second,
    w_first_held,
    w_second_held,
    feats,
    history,
    send_index,
    halo_index,
    hub_rows,
    tile_cols,
    tile_vals,
    send_feats,
    send_hist,
    send_hubs,
    send_fresh,
    slots_feats,
    slots_hist,
    hubs_first,
    hubs_second,
    all_grad_out,
    all_agg,
    hub_terms,
    hub_arrived,
    own_grad,
    gate_slope,
    dz_out,
    dz_in,
    agg_out,
    agg_in,
    first_terms,
    first_sent,
    first_in,
    second_terms,
    second_sent,
    second_in,
    rows_out,
    rows_in,
    local_sems,
    send_sems,
    recv_sems,
):
    group, dom = lax.axis_index("group"), lax.axis_index("dom")
    chips = doms // 2
    chip, core = dom // 2, dom % 2
    factor = 1.0 / math.sqrt(V_DEV * groups * doms)
    share = D // (groups * doms)
    dom_peers = [(dom + off) % doms for off in range(1, doms)]
    group_peers = [(group + off) % groups for off in range(1, groups)]
    sibling = dom + 1 - 2 * core
    chip_peers = [((chip + off) % chips) * 2 + core for off in range(1, chips)]
    chip_sources = [((chip + chips - off) % chips) * 2 + core for off in range(1, chips)]
    used = []

    loads = []
    for source, target in (
        (send_given, send_index),
        (hubs_given, hub_rows),
        (feats_given, feats),
        (history_given, history),
        (grad_given, all_grad_out.at[dom]),
        (halo_given, halo_index),
        (cols_given, tile_cols),
        (vals_given, tile_vals),
        (w_second, w_second_held),
        (w_first, w_first_held),
    ):
        loads.append(pltpu.make_async_copy(source, target, local_sems.at[len(loads)]))
        loads[-1].start()

    barrier = pltpu.get_barrier_semaphore()
    for peer in dom_peers:
        pl.semaphore_signal(
            barrier, inc=1, device_id=(group, peer), device_id_type=pl.DeviceIdType.MESH
        )
    for peer in group_peers:
        pl.semaphore_signal(
            barrier, inc=1, device_id=(peer, dom), device_id_type=pl.DeviceIdType.MESH
        )

    def send(source, target, to_group, to_dom):
        copy = pltpu.make_async_remote_copy(
            src_ref=source,
            dst_ref=target,
            send_sem=send_sems.at[len(used)],
            recv_sem=recv_sems.at[len(used)],
            device_id=(to_group, to_dom),
            device_id_type=pl.DeviceIdType.MESH,
        )
        used.append(copy)
        copy.start()
        return copy

    def to_doms(source, target):
        return [send(source.at[peer], target.at[dom], group, peer) for peer in dom_peers]

    def to_groups(source, target):
        return [send(source.at[peer], target.at[group], peer, dom) for peer in group_peers]

    def share_to_groups(source, target):
        return [send(source, target.at[group], peer, dom) for peer in group_peers]

    def to_chips(source, target):
        near = send(source, target.at[dom], group, sibling)
        return near, [send(source, target.at[dom], group, peer) for peer in chip_peers]

    def forward(far, target):
        passed = []
        for copy, origin in zip(far, chip_sources):
            copy.wait_recv()
            passed.append(send(target.at[origin], target.at[origin], group, sibling))
        return passed

    def arrived(copies):
        for copy in copies:
            copy.wait_recv()

    lane_row = lax.broadcasted_iota(jnp.int32, (1, V_DEV), 1)
    cap, hub_count = send_index.shape[2], hub_rows.shape[1]
    loads[0].wait()
    routes = jnp.broadcast_to(
        send_index[0].astype(F32)[:, None, :], (doms, cap, cap)
    ).reshape(doms * cap, cap)
    at_lane = lax.broadcasted_iota(jnp.int32, (doms * cap, cap), 1)
    at_slot = lax.broadcasted_iota(jnp.int32, (doms * cap, cap), 0) % cap
    route_column = jnp.sum(jnp.where(at_lane == at_slot, routes, 0.0), axis=1, keepdims=True)
    route_pick = (lane_row.astype(F32) == route_column).astype(F32).astype(BF16)
    loads[1].wait()
    hub_square = jnp.broadcast_to(hub_rows[...].astype(F32), (hub_count, hub_count))
    diagonal = lax.broadcasted_iota(jnp.int32, (hub_count, hub_count), 0) == (
        lax.broadcasted_iota(jnp.int32, (hub_count, hub_count), 1)
    )
    hub_column = jnp.sum(jnp.where(diagonal, hub_square, 0.0), axis=1, keepdims=True)
    hub_chosen = (lane_row.astype(F32) == hub_column).astype(F32)
    hub_pick = hub_chosen.astype(BF16)
    hub_spread = jnp.concatenate([hub_chosen] * groups, axis=0).T.astype(BF16)
    loads[2].wait()

    send_feats[...] = dot(route_pick, feats[...]).astype(BF16).reshape(send_feats.shape)
    send_hubs[...] = dot(hub_pick, feats[...]).astype(BF16)
    pl.semaphore_wait(barrier, doms - 1 + groups - 1)
    feat_copies = to_doms(send_feats, slots_feats)
    hub_copies = share_to_groups(send_hubs, hubs_first)
    slots_feats[dom] = send_feats[dom]
    hubs_first[group] = send_hubs[...]
    loads[3].wait()
    send_hist[...] = dot(route_pick, history[...]).astype(BF16).reshape(send_hist.shape)
    hist_copies = to_doms(send_hist, slots_hist)
    slots_hist[dom] = send_hist[dom]
    loads[4].wait()
    grad_near, grad_far = to_chips(all_grad_out.at[dom], all_grad_out)

    places = 3 * V_DEV
    place_of = lax.broadcasted_iota(jnp.int32, (places, V_DEV), 0)
    weights = jnp.zeros((V_DEV, places), F32)
    halo_tiles = HALO // TILE
    for load in loads[5:8]:
        load.wait()
    for tile in range(tile_vals.shape[1]):
        column = tile_cols[0:1, tile : tile + 1]
        target = jnp.where(column == 0, lane_row, lane_row + 2 * V_DEV)
        for halo in range(halo_tiles):
            slot = halo_index[halo * TILE : (halo + 1) * TILE].reshape(1, TILE) + V_DEV
            target = jnp.where(column == halo + 1, slot, target)
        chosen = (place_of == target).astype(F32).astype(BF16)
        weights = weights + dot(tile_vals[0, tile], chosen, (1, 1))
    own, slot, hub = (weights[:, n * V_DEV : (n + 1) * V_DEV] for n in range(3))
    own_pair, slot_pair, hub_pair = halves(own), halves(slot), halves(hub)

    loads[8].wait()
    agg_grad = dot(all_grad_out[dom], w_second_held[...], (1, 1)).astype(BF16)
    hub_terms[...] = apply_halves(halves(hub.T), agg_grad).astype(BF16).reshape(hub_terms.shape)
    term_copies = to_groups(hub_terms, hub_arrived)
    hub_arrived[group] = hub_terms[group]
    own_grad[...] = apply_halves(halves(own.T), agg_grad)

    first = apply_halves(own_pair, feats[...])
    arrived(feat_copies)
    first = first + apply_halves(slot_pair, slots_feats[...].reshape(V_DEV, D))
    arrived(hub_copies)
    first = first + apply_halves(hub_pair, hubs_first[...].reshape(V_DEV, D))
    agg_first = first.astype(BF16)
    all_agg[dom] = agg_first
    agg_near, agg_far = to_chips(all_agg.at[dom], all_agg)

    loads[9].wait()
    z_first = dot(agg_first, w_first_held[...])
    gate = 1.0 / (1.0 + jnp.exp(-z_first))
    fresh = (z_first * gate).astype(BF16)
    new_history[...] = fresh
    send_fresh[...] = dot(hub_pick, fresh).astype(BF16)
    fresh_copies = share_to_groups(send_fresh, hubs_second)
    hubs_second[group] = send_fresh[...]
    gate_slope[...] = gate * (1.0 + z_first * (1.0 - gate))

    arrived(term_copies)
    vertex_grad = own_grad[...] + dot(hub_spread, hub_arrived[...].reshape(V_DEV, D))
    embed_grad[...] = vertex_grad.astype(BF16)
    own_grad[...] = vertex_grad * gate_slope[...]
    for g in range(groups):
        for d in range(0, doms * share, TILE):
            start = g * doms * share + d
            block = own_grad[:, start : start + TILE].T.astype(BF16)
            for piece in range(TILE // share):
                dz_out[d // share + piece, g * share : (g + 1) * share, :] = block[
                    piece * share : (piece + 1) * share
                ]
    dz_copies = to_doms(dz_out, dz_in)
    dz_in[dom] = dz_out[dom]

    arrived(hist_copies)
    second = apply_halves(own_pair, new_history[...])
    second = second + apply_halves(slot_pair, slots_hist[...].reshape(V_DEV, D))
    arrived(fresh_copies)
    second = second + apply_halves(hub_pair, hubs_second[...].reshape(V_DEV, D))
    wide = D // doms
    for d in range(doms):
        agg_out[d] = second[:, d * wide : (d + 1) * wide].T.astype(BF16)
    agg_copies = to_doms(agg_out, agg_in)
    agg_in[dom] = agg_out[dom]

    grad_passed = forward(grad_far, all_grad_out)
    agg_passed = forward(agg_far, all_agg)
    arrived([grad_near] + grad_passed)
    arrived(agg_copies)
    blocks = jnp.concatenate([agg_in[d] for d in range(doms)], axis=1)
    total = dot(blocks, all_grad_out[...].reshape(doms * V_DEV, D))
    per_group = D // groups
    for g in range(groups):
        for n in range(0, per_group, TILE):
            start = g * per_group + n
            block = total[:, start : start + TILE].T
            second_terms[g, n : n + TILE, :] = block
            second_sent[g, n : n + TILE, :] = block.astype(BF16)
    second_copies = to_groups(second_sent, second_in)

    arrived([agg_near] + agg_passed)
    arrived(dz_copies)
    blocks = jnp.concatenate([dz_in[d] for d in range(doms)], axis=1)
    total = dot(blocks, all_agg[...].reshape(doms * V_DEV, D))
    first_terms[...] = total.reshape(first_terms.shape)
    first_sent[...] = total.astype(BF16).reshape(first_sent.shape)
    first_copies = to_groups(first_sent, first_in)

    arrived(second_copies)
    second_in[group] = jnp.zeros(second_in.shape[1:], BF16)
    total = second_terms[group]
    for g in range(groups):
        total = total + second_in[g].astype(F32)
    rows_out[...] = (total * factor).reshape(rows_out.shape)
    row_copies = to_doms(rows_out, rows_in)
    rows_in[dom] = rows_out[dom]

    arrived(first_copies)
    first_in[group] = jnp.zeros(first_in.shape[1:], BF16)
    total = first_terms[group]
    for g in range(groups):
        total = total + first_in[g].astype(F32)
    grad_first[...] = total * factor

    arrived(row_copies)
    for d in range(doms):
        grad_second[:, d * wide : (d + 1) * wide] = rows_in[d]
    for copy in used:
        copy.wait_send()


def write_kernel(*refs):
    sems = refs[8]
    copies = [pltpu.make_async_copy(refs[n], refs[n + 4], sems.at[n]) for n in range(4)]
    for copy in copies:
        copy.start()
    for copy in copies:
        copy.wait()


def in_kernel(
    feats, history, grad_out, w_first, w_second, send_index, halo_index, hub_rows, tile_cols, tile_vals
):
    groups, doms = lax.axis_size("group"), lax.axis_size("dom")
    share = D // (groups * doms)
    cap, hubs = send_index.shape[2], hub_rows.shape[1]
    wide, per_group = D // doms, D // groups
    copies = 7 * (doms - 1) + 5 * (groups - 1)
    vmem = pl.BlockSpec(memory_space=pltpu.VMEM)
    hbm = pl.BlockSpec(memory_space=pltpu.HBM)
    held = pltpu.VMEM
    results = pl.pallas_call(
        functools.partial(window_kernel, groups, doms),
        out_shape=(
            jax.ShapeDtypeStruct((V_DEV, D), BF16),
            jax.ShapeDtypeStruct((V_DEV, D), BF16),
            jax.ShapeDtypeStruct((share, D), F32),
            jax.ShapeDtypeStruct((share, D), F32),
        ),
        in_specs=[hbm] * 10,
        out_specs=(vmem,) * 4,
        scratch_shapes=[
            held((D, D), BF16),
            held((D, D), BF16),
            held((V_DEV, D), BF16),
            held((V_DEV, D), BF16),
            held(send_index.shape, jnp.int32),
            held(halo_index.shape, jnp.int32),
            held(hub_rows.shape, jnp.int32),
            held(tile_cols.shape, jnp.int32),
            held(tile_vals.shape, BF16),
            held((doms, cap, D), BF16),
            held((doms, cap, D), BF16),
            held((hubs, D), BF16),
            held((hubs, D), BF16),
            held((doms, cap, D), BF16),
            held((doms, cap, D), BF16),
            held((groups, hubs, D), BF16),
            held((groups, hubs, D), BF16),
            held((doms, V_DEV, D), BF16),
            held((doms, V_DEV, D), BF16),
            held((groups, hubs, D), BF16),
            held((groups, hubs, D), BF16),
            held((V_DEV, D), F32),
            held((V_DEV, D), F32),
            held((doms, groups * share, V_DEV), BF16),
            held((doms, groups * share, V_DEV), BF16),
            held((doms, wide, V_DEV), BF16),
            held((doms, wide, V_DEV), BF16),
            held((groups, share, D), F32),
            held((groups, share, D), BF16),
            held((groups, share, D), BF16),
            held((groups, per_group, wide), F32),
            held((groups, per_group, wide), BF16),
            held((groups, per_group, wide), BF16),
            held((doms, share, wide), F32),
            held((doms, share, wide), F32),
            pltpu.SemaphoreType.DMA((10,)),
            pltpu.SemaphoreType.DMA((copies,)),
            pltpu.SemaphoreType.DMA((copies,)),
        ],
        compiler_params=pltpu.CompilerParams(
            collective_id=0, has_side_effects=True, vmem_limit_bytes=62 * 1024 * 1024
        ),
    )(
        feats,
        history,
        grad_out,
        w_first,
        w_second,
        send_index,
        halo_index,
        hub_rows,
        tile_cols,
        tile_vals,
    )
    return pl.pallas_call(
        write_kernel,
        out_shape=tuple(jax.ShapeDtypeStruct(part.shape, part.dtype) for part in results),
        in_specs=[pl.BlockSpec(memory_space=pl.ANY)] * 4,
        out_specs=(hbm,) * 4,
        scratch_shapes=[pltpu.SemaphoreType.DMA((4,))],
    )(*results)


def fits_kernel(groups, doms, cap, hubs):
    return (
        D % (groups * doms * 16) == 0
        and TILE % (D // (groups * doms)) == 0
        and D // doms == V_DEV
        and doms * cap == V_DEV
        and groups * hubs == V_DEV
    )


def window(*args):
    send_index, hub_rows = args[5], args[7]
    groups, doms = lax.axis_size("group"), lax.axis_size("dom")
    if fits_kernel(groups, doms, send_index.shape[2], hub_rows.shape[1]):
        return in_kernel(*args)
    return on_device(*args)


def solution(mesh):
    placed = (
        P(("group", "dom"), None),
        P(("group", "dom"), None),
        P(("group", "dom"), None),
        P(),
        P(),
        P(("group", "dom"), None, None),
        P(("group", "dom")),
        P(("group", "dom"), None),
        P(("group", "dom"), None),
        P(("group", "dom"), None, None, None),
    )
    return jax.shard_map(
        window,
        mesh=mesh,
        in_specs=placed,
        out_specs=(
            P(("group", "dom"), None),
            P(("group", "dom"), None),
            P(("group", "dom"), None),
            P(("group", "dom"), None),
        ),
        check_vma=False,
    )
```

```python
import functools
import math

import jax
import jax.numpy as jnp
from jax import lax
from jax.experimental import pallas as pl
from jax.experimental.pallas import tpu as pltpu
from jax.sharding import PartitionSpec as P

D = 1024
V_DEV = 128
TILE = 128
HALO = 512


def combine_tiles(own_rows, halo_rows, hub_panel, tile_cols, tile_vals):
    source = jnp.concatenate([own_rows, halo_rows, hub_panel], axis=0)
    feature_width = source.shape[1]
    picked = source.reshape(-1, tile_vals.shape[2], feature_width)[tile_cols]
    summed = jnp.einsum("rtij,rtjd->rid", tile_vals, picked, preferred_element_type=jnp.float32)
    return summed.reshape(-1, feature_width).astype(jnp.bfloat16)


def reduce_weight(left_rows, right_rows):
    groups, doms = lax.axis_size("group"), lax.axis_size("dom")
    factor = 1.0 / math.sqrt(left_rows.shape[0] * groups * doms)
    rows = left_rows.shape[0]
    gathered = lax.all_gather(right_rows, "dom", axis=0, tiled=True)
    by_dom = left_rows.reshape(rows, groups, doms, -1).transpose(2, 0, 1, 3).reshape(doms * rows, -1)
    columns = lax.all_to_all(by_dom, "dom", split_axis=0, concat_axis=0, tiled=True)
    product = lax.dot_general(
        columns, gathered, (((0,), (0,)), ((), ())), preferred_element_type=jnp.float32
    )
    summed = lax.psum_scatter(product, "group", scatter_dimension=0, tiled=True)
    return summed * factor


def on_device(
    feats,
    history,
    grad_out,
    w_first,
    w_second,
    send_index,
    halo_index,
    hub_rows,
    tile_cols,
    tile_vals,
):
    routes = send_index[0]
    owned_hubs = hub_rows[0]
    feat_slots = lax.all_to_all(feats[routes], "dom", split_axis=0, concat_axis=0, tiled=True)
    feat_halo = feat_slots.reshape(-1, D)[halo_index]
    hub_first = lax.all_gather(feats[owned_hubs], "group", axis=0, tiled=True)
    agg_first = combine_tiles(feats, feat_halo, hub_first, tile_cols, tile_vals)
    z_first = jnp.dot(agg_first, w_first, preferred_element_type=jnp.float32)
    new_history = jax.nn.silu(z_first).astype(jnp.bfloat16)
    hist_slots = lax.all_to_all(history[routes], "dom", split_axis=0, concat_axis=0, tiled=True)
    hist_halo = hist_slots.reshape(-1, D)[halo_index]
    hub_second = lax.all_gather(new_history[owned_hubs], "group", axis=0, tiled=True)
    agg_second = combine_tiles(new_history, hist_halo, hub_second, tile_cols, tile_vals)
    grad_second = reduce_weight(grad_out, agg_second)
    agg_grad = lax.dot_general(
        grad_out, w_second, (((1,), (1,)), ((), ())), preferred_element_type=jnp.float32
    ).astype(jnp.bfloat16)
    source_tiles = (V_DEV + HALO + hub_second.shape[0]) // TILE
    tile_terms = jnp.einsum(
        "rtij,rid->rtjd",
        tile_vals,
        agg_grad.reshape(-1, TILE, D),
        preferred_element_type=jnp.float32,
    )
    selector = (
        tile_cols[:, :, None] == jnp.arange(source_tiles, dtype=jnp.int32)[None, None, :]
    ).astype(jnp.float32)
    spread = jnp.einsum(
        "rts,rtjd->sjd", selector, tile_terms, precision=lax.Precision.HIGHEST
    ).reshape(-1, D)
    own_grad = spread[:V_DEV]
    hub_grad = lax.psum_scatter(spread[V_DEV + HALO :], "group", scatter_dimension=0, tiled=True)
    vertex_grad = own_grad.at[owned_hubs].add(hub_grad)
    gate_value = jax.nn.sigmoid(z_first)
    dz_first = (vertex_grad * gate_value * (1.0 + z_first * (1.0 - gate_value))).astype(
        jnp.bfloat16
    )
    grad_first = reduce_weight(dz_first, agg_first)
    return (new_history, vertex_grad.astype(jnp.bfloat16), grad_first, grad_second)


BF16, F32 = jnp.bfloat16, jnp.float32


def dot(left, right, contract=(1, 0)):
    dims = (((contract[0],), (contract[1],)), ((), ()))
    return lax.dot_general(left, right, dims, preferred_element_type=F32)


def halves(weights):
    high = weights.astype(BF16)
    low = (weights - high.astype(F32)).astype(BF16)
    return jnp.concatenate([high, low], axis=0)


def apply_halves(pair, rows):
    both = dot(pair, rows)
    count = pair.shape[0] // 2
    return both[:count] + both[count:]


def window_kernel(
    groups,
    doms,
    feats_given,
    history_given,
    grad_given,
    w_first,
    w_second,
    send_given,
    halo_given,
    hubs_given,
    cols_given,
    vals_given,
    new_history,
    embed_grad,
    grad_first,
    grad_second,
    w_first_held,
    w_second_held,
    feats,
    history,
    send_index,
    halo_index,
    hub_rows,
    tile_cols,
    tile_vals,
    send_feats,
    send_hist,
    send_hubs,
    send_fresh,
    slots_feats,
    slots_hist,
    hubs_first,
    hubs_second,
    all_grad_out,
    all_agg,
    hub_terms,
    hub_arrived,
    own_grad,
    gate_slope,
    dz_out,
    dz_in,
    agg_out,
    agg_in,
    first_terms,
    first_sent,
    first_in,
    second_terms,
    second_sent,
    second_in,
    rows_out,
    rows_in,
    local_sems,
    send_sems,
    recv_sems,
):
    group, dom = lax.axis_index("group"), lax.axis_index("dom")
    chip, core = dom // 2, dom % 2
    factor = 1.0 / math.sqrt(V_DEV * groups * doms)
    share = D // (groups * doms)
    dom_peers = [(dom + off) % doms for off in range(1, doms)]
    group_peers = [(group + off) % groups for off in range(1, groups)]
    sibling = dom + 1 - 2 * core
    beside = (chip + 1 - 2 * (chip % 2)) * 2 + core
    across = ((chip + 2) % 4) * 2 + core
    opposite = (3 - chip) * 2 + core
    used = []

    loads = []
    for source, target in (
        (send_given, send_index),
        (hubs_given, hub_rows),
        (feats_given, feats),
        (history_given, history),
        (grad_given, all_grad_out.at[dom]),
        (halo_given, halo_index),
        (cols_given, tile_cols),
        (vals_given, tile_vals),
        (w_second, w_second_held),
        (w_first, w_first_held),
    ):
        loads.append(pltpu.make_async_copy(source, target, local_sems.at[len(loads)]))
        loads[-1].start()

    barrier = pltpu.get_barrier_semaphore()
    for peer in dom_peers:
        pl.semaphore_signal(
            barrier, inc=1, device_id=(group, peer), device_id_type=pl.DeviceIdType.MESH
        )
    for peer in group_peers:
        pl.semaphore_signal(
            barrier, inc=1, device_id=(peer, dom), device_id_type=pl.DeviceIdType.MESH
        )

    def send(source, target, to_group, to_dom):
        copy = pltpu.make_async_remote_copy(
            src_ref=source,
            dst_ref=target,
            send_sem=send_sems.at[len(used)],
            recv_sem=recv_sems.at[len(used)],
            device_id=(to_group, to_dom),
            device_id_type=pl.DeviceIdType.MESH,
        )
        used.append(copy)
        copy.start()
        return copy

    def to_doms(source, target):
        return [send(source.at[peer], target.at[dom], group, peer) for peer in dom_peers]

    def to_groups(source, target):
        return [send(source.at[peer], target.at[group], peer, dom) for peer in group_peers]

    def share_to_groups(source, target):
        return [send(source, target.at[group], peer, dom) for peer in group_peers]

    def to_near(target):
        block = target.at[dom]
        return [send(block, block, group, peer) for peer in (sibling, beside, across)]

    def relay(near, target):
        near[1].wait_recv()
        block = target.at[beside]
        upper = target.at[beside, pl.ds(0, V_DEV // 2)]
        parts = [send(upper, upper, group, across)]
        passed = [send(block, block, group, sibling)]
        near[2].wait_recv()
        block = target.at[across]
        lower = target.at[across, pl.ds(V_DEV // 2, V_DEV // 2)]
        parts.append(send(lower, lower, group, beside))
        passed.append(send(block, block, group, sibling))
        return parts, passed

    def finish(near, parts, passed, target):
        arrived(parts)
        block = target.at[opposite]
        arrived([near[0]] + passed + [send(block, block, group, sibling)])

    def arrived(copies):
        for copy in copies:
            copy.wait_recv()

    lane_row = lax.broadcasted_iota(jnp.int32, (1, V_DEV), 1)
    cap, hub_count = send_index.shape[2], hub_rows.shape[1]
    loads[0].wait()
    routes = jnp.broadcast_to(
        send_index[0].astype(F32)[:, None, :], (doms, cap, cap)
    ).reshape(doms * cap, cap)
    at_lane = lax.broadcasted_iota(jnp.int32, (doms * cap, cap), 1)
    at_slot = lax.broadcasted_iota(jnp.int32, (doms * cap, cap), 0) % cap
    route_column = jnp.sum(jnp.where(at_lane == at_slot, routes, 0.0), axis=1, keepdims=True)
    route_pick = (lane_row.astype(F32) == route_column).astype(F32).astype(BF16)
    loads[1].wait()
    hub_square = jnp.broadcast_to(hub_rows[...].astype(F32), (hub_count, hub_count))
    diagonal = lax.broadcasted_iota(jnp.int32, (hub_count, hub_count), 0) == (
        lax.broadcasted_iota(jnp.int32, (hub_count, hub_count), 1)
    )
    hub_column = jnp.sum(jnp.where(diagonal, hub_square, 0.0), axis=1, keepdims=True)
    hub_chosen = (lane_row.astype(F32) == hub_column).astype(F32)
    hub_pick = hub_chosen.astype(BF16)
    hub_spread = jnp.concatenate([hub_chosen] * groups, axis=0).T.astype(BF16)
    loads[2].wait()

    send_feats[...] = dot(route_pick, feats[...]).astype(BF16).reshape(send_feats.shape)
    send_hubs[...] = dot(hub_pick, feats[...]).astype(BF16)
    pl.semaphore_wait(barrier, doms - 1 + groups - 1)
    feat_copies = to_doms(send_feats, slots_feats)
    hub_copies = share_to_groups(send_hubs, hubs_first)
    slots_feats[dom] = send_feats[dom]
    hubs_first[group] = send_hubs[...]
    loads[3].wait()
    send_hist[...] = dot(route_pick, history[...]).astype(BF16).reshape(send_hist.shape)
    hist_copies = to_doms(send_hist, slots_hist)
    slots_hist[dom] = send_hist[dom]
    loads[4].wait()
    grad_near = to_near(all_grad_out)

    places = 3 * V_DEV
    place_of = lax.broadcasted_iota(jnp.int32, (places, V_DEV), 0)
    weights = jnp.zeros((V_DEV, places), F32)
    halo_tiles = HALO // TILE
    for load in loads[5:8]:
        load.wait()
    for tile in range(tile_vals.shape[1]):
        column = tile_cols[0:1, tile : tile + 1]
        target = jnp.where(column == 0, lane_row, lane_row + 2 * V_DEV)
        for halo in range(halo_tiles):
            slot = halo_index[halo * TILE : (halo + 1) * TILE].reshape(1, TILE) + V_DEV
            target = jnp.where(column == halo + 1, slot, target)
        chosen = (place_of == target).astype(F32).astype(BF16)
        weights = weights + dot(tile_vals[0, tile], chosen, (1, 1))
    own, slot, hub = (weights[:, n * V_DEV : (n + 1) * V_DEV] for n in range(3))
    own_pair, slot_pair, hub_pair = halves(own), halves(slot), halves(hub)

    loads[8].wait()
    agg_grad = dot(all_grad_out[dom], w_second_held[...], (1, 1)).astype(BF16)
    hub_terms[...] = apply_halves(halves(hub.T), agg_grad).astype(BF16).reshape(hub_terms.shape)
    term_copies = to_groups(hub_terms, hub_arrived)
    hub_arrived[group] = hub_terms[group]
    own_grad[...] = apply_halves(halves(own.T), agg_grad)

    first = apply_halves(own_pair, feats[...])
    arrived(feat_copies)
    first = first + apply_halves(slot_pair, slots_feats[...].reshape(V_DEV, D))
    arrived(hub_copies)
    first = first + apply_halves(hub_pair, hubs_first[...].reshape(V_DEV, D))
    agg_first = first.astype(BF16)
    all_agg[dom] = agg_first
    agg_near = to_near(all_agg)

    loads[9].wait()
    z_first = dot(agg_first, w_first_held[...])
    gate = 1.0 / (1.0 + jnp.exp(-z_first))
    fresh = (z_first * gate).astype(BF16)
    new_history[...] = fresh
    send_fresh[...] = dot(hub_pick, fresh).astype(BF16)
    fresh_copies = share_to_groups(send_fresh, hubs_second)
    hubs_second[group] = send_fresh[...]
    gate_slope[...] = gate * (1.0 + z_first * (1.0 - gate))

    arrived(term_copies)
    vertex_grad = own_grad[...] + dot(hub_spread, hub_arrived[...].reshape(V_DEV, D))
    embed_grad[...] = vertex_grad.astype(BF16)
    own_grad[...] = vertex_grad * gate_slope[...]
    for g in range(groups):
        for d in range(0, doms * share, TILE):
            start = g * doms * share + d
            block = own_grad[:, start : start + TILE].T.astype(BF16)
            for piece in range(TILE // share):
                dz_out[d // share + piece, g * share : (g + 1) * share, :] = block[
                    piece * share : (piece + 1) * share
                ]
    dz_copies = to_doms(dz_out, dz_in)
    dz_in[dom] = dz_out[dom]
    grad_parts, grad_passed = relay(grad_near, all_grad_out)

    arrived(hist_copies)
    second = apply_halves(own_pair, new_history[...])
    second = second + apply_halves(slot_pair, slots_hist[...].reshape(V_DEV, D))
    arrived(fresh_copies)
    second = second + apply_halves(hub_pair, hubs_second[...].reshape(V_DEV, D))
    wide = D // doms
    for d in range(doms):
        agg_out[d] = second[:, d * wide : (d + 1) * wide].T.astype(BF16)
    agg_copies = to_doms(agg_out, agg_in)
    agg_in[dom] = agg_out[dom]

    finish(grad_near, grad_parts, grad_passed, all_grad_out)
    agg_parts, agg_passed = relay(agg_near, all_agg)
    arrived(agg_copies)
    blocks = jnp.concatenate([agg_in[d] for d in range(doms)], axis=1)
    total = dot(blocks, all_grad_out[...].reshape(doms * V_DEV, D))
    per_group = D // groups
    for g in range(groups):
        for n in range(0, per_group, TILE):
            start = g * per_group + n
            block = total[:, start : start + TILE].T
            second_terms[g, n : n + TILE, :] = block
            second_sent[g, n : n + TILE, :] = block.astype(BF16)
    second_copies = to_groups(second_sent, second_in)

    finish(agg_near, agg_parts, agg_passed, all_agg)
    arrived(dz_copies)
    blocks = jnp.concatenate([dz_in[d] for d in range(doms)], axis=1)
    total = dot(blocks, all_agg[...].reshape(doms * V_DEV, D))
    first_terms[...] = total.reshape(first_terms.shape)
    first_sent[...] = total.astype(BF16).reshape(first_sent.shape)
    first_copies = to_groups(first_sent, first_in)

    arrived(second_copies)
    second_in[group] = jnp.zeros(second_in.shape[1:], BF16)
    total = second_terms[group]
    for g in range(groups):
        total = total + second_in[g].astype(F32)
    rows_out[...] = (total * factor).reshape(rows_out.shape)
    row_copies = to_doms(rows_out, rows_in)
    rows_in[dom] = rows_out[dom]

    arrived(first_copies)
    first_in[group] = jnp.zeros(first_in.shape[1:], BF16)
    total = first_terms[group]
    for g in range(groups):
        total = total + first_in[g].astype(F32)
    grad_first[...] = total * factor

    arrived(row_copies)
    for d in range(doms):
        grad_second[:, d * wide : (d + 1) * wide] = rows_in[d]
    for copy in used:
        copy.wait_send()


def in_kernel(
    feats, history, grad_out, w_first, w_second, send_index, halo_index, hub_rows, tile_cols, tile_vals
):
    groups, doms = lax.axis_size("group"), lax.axis_size("dom")
    share = D // (groups * doms)
    cap, hubs = send_index.shape[2], hub_rows.shape[1]
    wide, per_group = D // doms, D // groups
    copies = 5 * (doms - 1) + 5 * (groups - 1) + 16
    vmem = pl.BlockSpec(memory_space=pltpu.VMEM)
    hbm = pl.BlockSpec(memory_space=pltpu.HBM)
    held = pltpu.VMEM
    return pl.pallas_call(
        functools.partial(window_kernel, groups, doms),
        out_shape=(
            jax.ShapeDtypeStruct((V_DEV, D), BF16),
            jax.ShapeDtypeStruct((V_DEV, D), BF16),
            jax.ShapeDtypeStruct((share, D), F32),
            jax.ShapeDtypeStruct((share, D), F32),
        ),
        in_specs=[hbm] * 10,
        out_specs=(vmem,) * 4,
        scratch_shapes=[
            held((D, D), BF16),
            held((D, D), BF16),
            held((V_DEV, D), BF16),
            held((V_DEV, D), BF16),
            held(send_index.shape, jnp.int32),
            held(halo_index.shape, jnp.int32),
            held(hub_rows.shape, jnp.int32),
            held(tile_cols.shape, jnp.int32),
            held(tile_vals.shape, BF16),
            held((doms, cap, D), BF16),
            held((doms, cap, D), BF16),
            held((hubs, D), BF16),
            held((hubs, D), BF16),
            held((doms, cap, D), BF16),
            held((doms, cap, D), BF16),
            held((groups, hubs, D), BF16),
            held((groups, hubs, D), BF16),
            held((doms, V_DEV, D), BF16),
            held((doms, V_DEV, D), BF16),
            held((groups, hubs, D), BF16),
            held((groups, hubs, D), BF16),
            held((V_DEV, D), F32),
            held((V_DEV, D), F32),
            held((doms, groups * share, V_DEV), BF16),
            held((doms, groups * share, V_DEV), BF16),
            held((doms, wide, V_DEV), BF16),
            held((doms, wide, V_DEV), BF16),
            held((groups, share, D), F32),
            held((groups, share, D), BF16),
            held((groups, share, D), BF16),
            held((groups, per_group, wide), F32),
            held((groups, per_group, wide), BF16),
            held((groups, per_group, wide), BF16),
            held((doms, share, wide), F32),
            held((doms, share, wide), F32),
            pltpu.SemaphoreType.DMA((10,)),
            pltpu.SemaphoreType.DMA((copies,)),
            pltpu.SemaphoreType.DMA((copies,)),
        ],
        compiler_params=pltpu.CompilerParams(
            collective_id=0, has_side_effects=True, vmem_limit_bytes=60 * 1024 * 1024
        ),
    )(
        feats,
        history,
        grad_out,
        w_first,
        w_second,
        send_index,
        halo_index,
        hub_rows,
        tile_cols,
        tile_vals,
    )


def fits_kernel(groups, doms, cap, hubs):
    return (
        D % (groups * doms * 16) == 0
        and TILE % (D // (groups * doms)) == 0
        and doms == 8
        and D // doms == V_DEV
        and doms * cap == V_DEV
        and groups * hubs == V_DEV
    )


def window(*args):
    send_index, hub_rows = args[5], args[7]
    groups, doms = lax.axis_size("group"), lax.axis_size("dom")
    if fits_kernel(groups, doms, send_index.shape[2], hub_rows.shape[1]):
        return in_kernel(*args)
    return on_device(*args)


def solution(mesh):
    placed = (
        P(("group", "dom"), None),
        P(("group", "dom"), None),
        P(("group", "dom"), None),
        P(),
        P(),
        P(("group", "dom"), None, None),
        P(("group", "dom")),
        P(("group", "dom"), None),
        P(("group", "dom"), None),
        P(("group", "dom"), None, None, None),
    )
    return jax.shard_map(
        window,
        mesh=mesh,
        in_specs=placed,
        out_specs=(
            P(("group", "dom"), None),
            P(("group", "dom"), None),
            P(("group", "dom"), None),
            P(("group", "dom"), None),
        ),
        check_vma=False,
    )
```

```python
import functools
import math

import jax
import jax.numpy as jnp
from jax import lax
from jax.experimental import pallas as pl
from jax.experimental.pallas import tpu as pltpu
from jax.sharding import PartitionSpec as P

D = 1024
V_DEV = 128
TILE = 128
HALO = 512


def combine_tiles(own_rows, halo_rows, hub_panel, tile_cols, tile_vals):
    source = jnp.concatenate([own_rows, halo_rows, hub_panel], axis=0)
    feature_width = source.shape[1]
    picked = source.reshape(-1, tile_vals.shape[2], feature_width)[tile_cols]
    summed = jnp.einsum("rtij,rtjd->rid", tile_vals, picked, preferred_element_type=jnp.float32)
    return summed.reshape(-1, feature_width).astype(jnp.bfloat16)


def reduce_weight(left_rows, right_rows):
    groups, doms = lax.axis_size("group"), lax.axis_size("dom")
    factor = 1.0 / math.sqrt(left_rows.shape[0] * groups * doms)
    rows = left_rows.shape[0]
    gathered = lax.all_gather(right_rows, "dom", axis=0, tiled=True)
    by_dom = left_rows.reshape(rows, groups, doms, -1).transpose(2, 0, 1, 3).reshape(doms * rows, -1)
    columns = lax.all_to_all(by_dom, "dom", split_axis=0, concat_axis=0, tiled=True)
    product = lax.dot_general(
        columns, gathered, (((0,), (0,)), ((), ())), preferred_element_type=jnp.float32
    )
    summed = lax.psum_scatter(product, "group", scatter_dimension=0, tiled=True)
    return summed * factor


def on_device(
    feats,
    history,
    grad_out,
    w_first,
    w_second,
    send_index,
    halo_index,
    hub_rows,
    tile_cols,
    tile_vals,
):
    routes = send_index[0]
    owned_hubs = hub_rows[0]
    feat_slots = lax.all_to_all(feats[routes], "dom", split_axis=0, concat_axis=0, tiled=True)
    feat_halo = feat_slots.reshape(-1, D)[halo_index]
    hub_first = lax.all_gather(feats[owned_hubs], "group", axis=0, tiled=True)
    agg_first = combine_tiles(feats, feat_halo, hub_first, tile_cols, tile_vals)
    z_first = jnp.dot(agg_first, w_first, preferred_element_type=jnp.float32)
    new_history = jax.nn.silu(z_first).astype(jnp.bfloat16)
    hist_slots = lax.all_to_all(history[routes], "dom", split_axis=0, concat_axis=0, tiled=True)
    hist_halo = hist_slots.reshape(-1, D)[halo_index]
    hub_second = lax.all_gather(new_history[owned_hubs], "group", axis=0, tiled=True)
    agg_second = combine_tiles(new_history, hist_halo, hub_second, tile_cols, tile_vals)
    grad_second = reduce_weight(grad_out, agg_second)
    agg_grad = lax.dot_general(
        grad_out, w_second, (((1,), (1,)), ((), ())), preferred_element_type=jnp.float32
    ).astype(jnp.bfloat16)
    source_tiles = (V_DEV + HALO + hub_second.shape[0]) // TILE
    tile_terms = jnp.einsum(
        "rtij,rid->rtjd",
        tile_vals,
        agg_grad.reshape(-1, TILE, D),
        preferred_element_type=jnp.float32,
    )
    selector = (
        tile_cols[:, :, None] == jnp.arange(source_tiles, dtype=jnp.int32)[None, None, :]
    ).astype(jnp.float32)
    spread = jnp.einsum(
        "rts,rtjd->sjd", selector, tile_terms, precision=lax.Precision.HIGHEST
    ).reshape(-1, D)
    own_grad = spread[:V_DEV]
    hub_grad = lax.psum_scatter(spread[V_DEV + HALO :], "group", scatter_dimension=0, tiled=True)
    vertex_grad = own_grad.at[owned_hubs].add(hub_grad)
    gate_value = jax.nn.sigmoid(z_first)
    dz_first = (vertex_grad * gate_value * (1.0 + z_first * (1.0 - gate_value))).astype(
        jnp.bfloat16
    )
    grad_first = reduce_weight(dz_first, agg_first)
    return (new_history, vertex_grad.astype(jnp.bfloat16), grad_first, grad_second)


BF16, F32 = jnp.bfloat16, jnp.float32


def dot(left, right, contract=(1, 0)):
    dims = (((contract[0],), (contract[1],)), ((), ()))
    return lax.dot_general(left, right, dims, preferred_element_type=F32)


def halves(weights):
    high = weights.astype(BF16)
    low = (weights - high.astype(F32)).astype(BF16)
    return jnp.concatenate([high, low], axis=0)


def apply_halves(pair, rows):
    both = dot(pair, rows)
    count = pair.shape[0] // 2
    return both[:count] + both[count:]


def window_kernel(
    groups,
    doms,
    feats_given,
    history_given,
    grad_given,
    w_first,
    w_second,
    send_given,
    halo_given,
    hubs_given,
    cols_given,
    vals_given,
    new_history,
    embed_grad,
    grad_first,
    grad_second,
    w_first_held,
    w_second_held,
    feats,
    history,
    send_index,
    halo_index,
    hub_rows,
    tile_cols,
    tile_vals,
    send_feats,
    send_hist,
    send_hubs,
    send_fresh,
    slots_feats,
    slots_hist,
    hubs_first,
    hubs_second,
    all_grad_out,
    all_agg,
    hub_terms,
    hub_arrived,
    own_grad,
    gate_slope,
    dz_out,
    dz_in,
    agg_out,
    agg_in,
    first_terms,
    first_sent,
    first_in,
    second_terms,
    second_sent,
    second_in,
    rows_out,
    rows_in,
    local_sems,
    send_sems,
    recv_sems,
):
    group, dom = lax.axis_index("group"), lax.axis_index("dom")
    chip, core = dom // 2, dom % 2
    factor = 1.0 / math.sqrt(V_DEV * groups * doms)
    share = D // (groups * doms)
    dom_peers = [(dom + off) % doms for off in range(1, doms)]
    group_peers = [(group + off) % groups for off in range(1, groups)]
    sibling = dom + 1 - 2 * core
    beside = (chip + 1 - 2 * (chip % 2)) * 2 + core
    across = ((chip + 2) % 4) * 2 + core
    opposite = (3 - chip) * 2 + core
    used = []

    barrier = pltpu.get_barrier_semaphore()
    for peer in dom_peers:
        pl.semaphore_signal(
            barrier, inc=1, device_id=(group, peer), device_id_type=pl.DeviceIdType.MESH
        )
    for peer in group_peers:
        pl.semaphore_signal(
            barrier, inc=1, device_id=(peer, dom), device_id_type=pl.DeviceIdType.MESH
        )

    loads = []
    for source, target in (
        (send_given, send_index),
        (hubs_given, hub_rows),
        (feats_given, feats),
        (history_given, history),
        (grad_given, all_grad_out.at[dom]),
        (halo_given, halo_index),
        (cols_given, tile_cols),
        (vals_given, tile_vals),
        (w_second, w_second_held),
        (w_first, w_first_held),
    ):
        loads.append(pltpu.make_async_copy(source, target, local_sems.at[len(loads)]))
        loads[-1].start()

    def send(source, target, to_group, to_dom):
        copy = pltpu.make_async_remote_copy(
            src_ref=source,
            dst_ref=target,
            send_sem=send_sems.at[len(used)],
            recv_sem=recv_sems.at[len(used)],
            device_id=(to_group, to_dom),
            device_id_type=pl.DeviceIdType.MESH,
        )
        used.append(copy)
        copy.start()
        return copy

    def to_doms(source, target):
        return [send(source.at[peer], target.at[dom], group, peer) for peer in dom_peers]

    def to_groups(source, target):
        return [send(source.at[peer], target.at[group], peer, dom) for peer in group_peers]

    def share_to_groups(source, target):
        return [send(source, target.at[group], peer, dom) for peer in group_peers]

    def to_near(target):
        block = target.at[dom]
        return [send(block, block, group, peer) for peer in (sibling, beside, across)]

    def relay(near, target):
        near[1].wait_recv()
        block = target.at[beside]
        upper = target.at[beside, pl.ds(0, V_DEV // 2)]
        parts = [send(upper, upper, group, across)]
        passed = [send(block, block, group, sibling)]
        near[2].wait_recv()
        block = target.at[across]
        lower = target.at[across, pl.ds(V_DEV // 2, V_DEV // 2)]
        parts.append(send(lower, lower, group, beside))
        passed.append(send(block, block, group, sibling))
        return parts, passed

    def finish(near, parts, passed, target):
        arrived(parts)
        block = target.at[opposite]
        arrived([near[0]] + passed + [send(block, block, group, sibling)])

    def arrived(copies):
        for copy in copies:
            copy.wait_recv()

    lane_row = lax.broadcasted_iota(jnp.int32, (1, V_DEV), 1)
    cap, hub_count = send_index.shape[2], hub_rows.shape[1]
    loads[0].wait()
    routes = jnp.broadcast_to(
        send_index[0].astype(F32)[:, None, :], (doms, cap, cap)
    ).reshape(doms * cap, cap)
    at_lane = lax.broadcasted_iota(jnp.int32, (doms * cap, cap), 1)
    at_slot = lax.broadcasted_iota(jnp.int32, (doms * cap, cap), 0) % cap
    route_column = jnp.sum(jnp.where(at_lane == at_slot, routes, 0.0), axis=1, keepdims=True)
    route_pick = (lane_row.astype(F32) == route_column).astype(F32).astype(BF16)
    loads[1].wait()
    hub_square = jnp.broadcast_to(hub_rows[...].astype(F32), (hub_count, hub_count))
    diagonal = lax.broadcasted_iota(jnp.int32, (hub_count, hub_count), 0) == (
        lax.broadcasted_iota(jnp.int32, (hub_count, hub_count), 1)
    )
    hub_column = jnp.sum(jnp.where(diagonal, hub_square, 0.0), axis=1, keepdims=True)
    hub_chosen = (lane_row.astype(F32) == hub_column).astype(F32)
    hub_pick = hub_chosen.astype(BF16)
    hub_spread = jnp.concatenate([hub_chosen] * groups, axis=0).T.astype(BF16)
    loads[2].wait()

    send_hubs[...] = dot(hub_pick, feats[...]).astype(BF16)
    pl.semaphore_wait(barrier, doms - 1 + groups - 1)
    hub_copies = share_to_groups(send_hubs, hubs_first)
    send_feats[...] = dot(route_pick, feats[...]).astype(BF16).reshape(send_feats.shape)
    feat_copies = to_doms(send_feats, slots_feats)
    slots_feats[dom] = send_feats[dom]
    hubs_first[group] = send_hubs[...]
    loads[3].wait()
    send_hist[...] = dot(route_pick, history[...]).astype(BF16).reshape(send_hist.shape)
    slots_hist[dom] = send_hist[dom]
    loads[4].wait()

    places = 3 * V_DEV
    place_of = lax.broadcasted_iota(jnp.int32, (places, V_DEV), 0)
    weights = jnp.zeros((V_DEV, places), F32)
    halo_tiles = HALO // TILE
    for load in loads[5:8]:
        load.wait()
    for tile in range(tile_vals.shape[1]):
        column = tile_cols[0:1, tile : tile + 1]
        target = jnp.where(column == 0, lane_row, lane_row + 2 * V_DEV)
        for halo in range(halo_tiles):
            slot = halo_index[halo * TILE : (halo + 1) * TILE].reshape(1, TILE) + V_DEV
            target = jnp.where(column == halo + 1, slot, target)
        chosen = (place_of == target).astype(F32).astype(BF16)
        weights = weights + dot(tile_vals[0, tile], chosen, (1, 1))
    own, slot, hub = (weights[:, n * V_DEV : (n + 1) * V_DEV] for n in range(3))
    own_pair, slot_pair, hub_pair = halves(own), halves(slot), halves(hub)

    loads[8].wait()
    agg_grad = dot(all_grad_out[dom], w_second_held[...], (1, 1)).astype(BF16)
    hub_terms[...] = apply_halves(halves(hub.T), agg_grad).astype(BF16).reshape(hub_terms.shape)
    hub_arrived[group] = hub_terms[group]
    own_grad[...] = apply_halves(halves(own.T), agg_grad)

    first = apply_halves(own_pair, feats[...])
    arrived(feat_copies)
    grad_near = to_near(all_grad_out)
    hist_copies = to_doms(send_hist, slots_hist)
    first = first + apply_halves(slot_pair, slots_feats[...].reshape(V_DEV, D))
    arrived(hub_copies)
    term_copies = to_groups(hub_terms, hub_arrived)
    first = first + apply_halves(hub_pair, hubs_first[...].reshape(V_DEV, D))
    agg_first = first.astype(BF16)
    all_agg[dom] = agg_first
    agg_near = to_near(all_agg)

    loads[9].wait()
    z_first = dot(agg_first, w_first_held[...])
    gate = 1.0 / (1.0 + jnp.exp(-z_first))
    fresh = (z_first * gate).astype(BF16)
    new_history[...] = fresh
    send_fresh[...] = dot(hub_pick, fresh).astype(BF16)
    fresh_copies = share_to_groups(send_fresh, hubs_second)
    hubs_second[group] = send_fresh[...]
    gate_slope[...] = gate * (1.0 + z_first * (1.0 - gate))

    arrived(term_copies)
    vertex_grad = own_grad[...] + dot(hub_spread, hub_arrived[...].reshape(V_DEV, D))
    embed_grad[...] = vertex_grad.astype(BF16)
    own_grad[...] = vertex_grad * gate_slope[...]
    for g in range(groups):
        for d in range(0, doms * share, TILE):
            start = g * doms * share + d
            block = own_grad[:, start : start + TILE].T.astype(BF16)
            for piece in range(TILE // share):
                dz_out[d // share + piece, g * share : (g + 1) * share, :] = block[
                    piece * share : (piece + 1) * share
                ]
    dz_copies = to_doms(dz_out, dz_in)
    dz_in[dom] = dz_out[dom]
    grad_parts, grad_passed = relay(grad_near, all_grad_out)

    arrived(hist_copies)
    second = apply_halves(own_pair, new_history[...])
    second = second + apply_halves(slot_pair, slots_hist[...].reshape(V_DEV, D))
    arrived(fresh_copies)
    second = second + apply_halves(hub_pair, hubs_second[...].reshape(V_DEV, D))
    wide = D // doms
    for d in range(doms):
        agg_out[d] = second[:, d * wide : (d + 1) * wide].T.astype(BF16)
    agg_copies = to_doms(agg_out, agg_in)
    agg_in[dom] = agg_out[dom]

    finish(grad_near, grad_parts, grad_passed, all_grad_out)
    agg_parts, agg_passed = relay(agg_near, all_agg)
    arrived(agg_copies)
    blocks = jnp.concatenate([agg_in[d] for d in range(doms)], axis=1)
    total = dot(blocks, all_grad_out[...].reshape(doms * V_DEV, D))
    per_group = D // groups
    for g in range(groups):
        for n in range(0, per_group, TILE):
            start = g * per_group + n
            block = total[:, start : start + TILE].T
            second_terms[g, n : n + TILE, :] = block
            second_sent[g, n : n + TILE, :] = block.astype(BF16)
    second_copies = to_groups(second_sent, second_in)

    finish(agg_near, agg_parts, agg_passed, all_agg)
    arrived(dz_copies)
    blocks = jnp.concatenate([dz_in[d] for d in range(doms)], axis=1)
    total = dot(blocks, all_agg[...].reshape(doms * V_DEV, D))
    first_terms[...] = total.reshape(first_terms.shape)
    first_sent[...] = total.astype(BF16).reshape(first_sent.shape)
    first_copies = to_groups(first_sent, first_in)

    arrived(second_copies)
    second_in[group] = jnp.zeros(second_in.shape[1:], BF16)
    total = second_terms[group]
    for g in range(groups):
        total = total + second_in[g].astype(F32)
    rows_out[...] = (total * factor).reshape(rows_out.shape)
    row_copies = to_doms(rows_out, rows_in)
    rows_in[dom] = rows_out[dom]

    arrived(first_copies)
    first_in[group] = jnp.zeros(first_in.shape[1:], BF16)
    total = first_terms[group]
    for g in range(groups):
        total = total + first_in[g].astype(F32)
    grad_first[...] = total * factor

    arrived(row_copies)
    for d in range(doms):
        grad_second[:, d * wide : (d + 1) * wide] = rows_in[d]
    for copy in used:
        copy.wait_send()


def write_kernel(*refs):
    given, written, staged, sems = refs[:4], refs[4:8], refs[8:12], refs[12]
    reads = [pltpu.make_async_copy(given[n], staged[n], sems.at[n]) for n in range(4)]
    writes = [pltpu.make_async_copy(staged[n], written[n], sems.at[n + 4]) for n in range(4)]
    for copy in reads:
        copy.start()
    for read, write in zip(reads, writes):
        read.wait()
        write.start()
    for copy in writes:
        copy.wait()


def in_kernel(
    feats, history, grad_out, w_first, w_second, send_index, halo_index, hub_rows, tile_cols, tile_vals
):
    groups, doms = lax.axis_size("group"), lax.axis_size("dom")
    share = D // (groups * doms)
    cap, hubs = send_index.shape[2], hub_rows.shape[1]
    wide, per_group = D // doms, D // groups
    copies = 5 * (doms - 1) + 5 * (groups - 1) + 16
    vmem = pl.BlockSpec(memory_space=pltpu.VMEM)
    hbm = pl.BlockSpec(memory_space=pltpu.HBM)
    held = pltpu.VMEM
    results = pl.pallas_call(
        functools.partial(window_kernel, groups, doms),
        out_shape=(
            jax.ShapeDtypeStruct((V_DEV, D), BF16),
            jax.ShapeDtypeStruct((V_DEV, D), BF16),
            jax.ShapeDtypeStruct((share, D), F32),
            jax.ShapeDtypeStruct((share, D), F32),
        ),
        in_specs=[hbm] * 10,
        out_specs=(vmem,) * 4,
        scratch_shapes=[
            held((D, D), BF16),
            held((D, D), BF16),
            held((V_DEV, D), BF16),
            held((V_DEV, D), BF16),
            held(send_index.shape, jnp.int32),
            held(halo_index.shape, jnp.int32),
            held(hub_rows.shape, jnp.int32),
            held(tile_cols.shape, jnp.int32),
            held(tile_vals.shape, BF16),
            held((doms, cap, D), BF16),
            held((doms, cap, D), BF16),
            held((hubs, D), BF16),
            held((hubs, D), BF16),
            held((doms, cap, D), BF16),
            held((doms, cap, D), BF16),
            held((groups, hubs, D), BF16),
            held((groups, hubs, D), BF16),
            held((doms, V_DEV, D), BF16),
            held((doms, V_DEV, D), BF16),
            held((groups, hubs, D), BF16),
            held((groups, hubs, D), BF16),
            held((V_DEV, D), F32),
            held((V_DEV, D), F32),
            held((doms, groups * share, V_DEV), BF16),
            held((doms, groups * share, V_DEV), BF16),
            held((doms, wide, V_DEV), BF16),
            held((doms, wide, V_DEV), BF16),
            held((groups, share, D), F32),
            held((groups, share, D), BF16),
            held((groups, share, D), BF16),
            held((groups, per_group, wide), F32),
            held((groups, per_group, wide), BF16),
            held((groups, per_group, wide), BF16),
            held((doms, share, wide), F32),
            held((doms, share, wide), F32),
            pltpu.SemaphoreType.DMA((10,)),
            pltpu.SemaphoreType.DMA((copies,)),
            pltpu.SemaphoreType.DMA((copies,)),
        ],
        compiler_params=pltpu.CompilerParams(
            collective_id=0, has_side_effects=True, vmem_limit_bytes=60 * 1024 * 1024
        ),
    )(
        feats,
        history,
        grad_out,
        w_first,
        w_second,
        send_index,
        halo_index,
        hub_rows,
        tile_cols,
        tile_vals,
    )
    shapes = [(part.shape, part.dtype) for part in results]
    return pl.pallas_call(
        write_kernel,
        out_shape=tuple(jax.ShapeDtypeStruct(*shape) for shape in shapes),
        in_specs=[pl.BlockSpec(memory_space=pl.ANY)] * 4,
        out_specs=(hbm,) * 4,
        scratch_shapes=[held(*shape) for shape in shapes] + [pltpu.SemaphoreType.DMA((8,))],
        compiler_params=pltpu.CompilerParams(vmem_limit_bytes=60 * 1024 * 1024),
    )(*results)


def fits_kernel(groups, doms, cap, hubs):
    return (
        D % (groups * doms * 16) == 0
        and TILE % (D // (groups * doms)) == 0
        and doms == 8
        and D // doms == V_DEV
        and doms * cap == V_DEV
        and groups * hubs == V_DEV
    )


def window(*args):
    send_index, hub_rows = args[5], args[7]
    groups, doms = lax.axis_size("group"), lax.axis_size("dom")
    if fits_kernel(groups, doms, send_index.shape[2], hub_rows.shape[1]):
        return in_kernel(*args)
    return on_device(*args)


def solution(mesh):
    placed = (
        P(("group", "dom"), None),
        P(("group", "dom"), None),
        P(("group", "dom"), None),
        P(),
        P(),
        P(("group", "dom"), None, None),
        P(("group", "dom")),
        P(("group", "dom"), None),
        P(("group", "dom"), None),
        P(("group", "dom"), None, None, None),
    )
    return jax.shard_map(
        window,
        mesh=mesh,
        in_specs=placed,
        out_specs=(
            P(("group", "dom"), None),
            P(("group", "dom"), None),
            P(("group", "dom"), None),
            P(("group", "dom"), None),
        ),
        check_vma=False,
    )
```

```python
import functools
import math

import jax
import jax.numpy as jnp
from jax import lax
from jax.experimental import pallas as pl
from jax.experimental.pallas import tpu as pltpu
from jax.sharding import PartitionSpec as P

D = 1024
V_DEV = 128
TILE = 128
HALO = 512


def combine_tiles(own_rows, halo_rows, hub_panel, tile_cols, tile_vals):
    source = jnp.concatenate([own_rows, halo_rows, hub_panel], axis=0)
    feature_width = source.shape[1]
    picked = source.reshape(-1, tile_vals.shape[2], feature_width)[tile_cols]
    summed = jnp.einsum("rtij,rtjd->rid", tile_vals, picked, preferred_element_type=jnp.float32)
    return summed.reshape(-1, feature_width).astype(jnp.bfloat16)


def reduce_weight(left_rows, right_rows):
    groups, doms = lax.axis_size("group"), lax.axis_size("dom")
    factor = 1.0 / math.sqrt(left_rows.shape[0] * groups * doms)
    rows = left_rows.shape[0]
    gathered = lax.all_gather(right_rows, "dom", axis=0, tiled=True)
    by_dom = left_rows.reshape(rows, groups, doms, -1).transpose(2, 0, 1, 3).reshape(doms * rows, -1)
    columns = lax.all_to_all(by_dom, "dom", split_axis=0, concat_axis=0, tiled=True)
    product = lax.dot_general(
        columns, gathered, (((0,), (0,)), ((), ())), preferred_element_type=jnp.float32
    )
    summed = lax.psum_scatter(product, "group", scatter_dimension=0, tiled=True)
    return summed * factor


def on_device(
    feats,
    history,
    grad_out,
    w_first,
    w_second,
    send_index,
    halo_index,
    hub_rows,
    tile_cols,
    tile_vals,
):
    routes = send_index[0]
    owned_hubs = hub_rows[0]
    feat_slots = lax.all_to_all(feats[routes], "dom", split_axis=0, concat_axis=0, tiled=True)
    feat_halo = feat_slots.reshape(-1, D)[halo_index]
    hub_first = lax.all_gather(feats[owned_hubs], "group", axis=0, tiled=True)
    agg_first = combine_tiles(feats, feat_halo, hub_first, tile_cols, tile_vals)
    z_first = jnp.dot(agg_first, w_first, preferred_element_type=jnp.float32)
    new_history = jax.nn.silu(z_first).astype(jnp.bfloat16)
    hist_slots = lax.all_to_all(history[routes], "dom", split_axis=0, concat_axis=0, tiled=True)
    hist_halo = hist_slots.reshape(-1, D)[halo_index]
    hub_second = lax.all_gather(new_history[owned_hubs], "group", axis=0, tiled=True)
    agg_second = combine_tiles(new_history, hist_halo, hub_second, tile_cols, tile_vals)
    grad_second = reduce_weight(grad_out, agg_second)
    agg_grad = lax.dot_general(
        grad_out, w_second, (((1,), (1,)), ((), ())), preferred_element_type=jnp.float32
    ).astype(jnp.bfloat16)
    source_tiles = (V_DEV + HALO + hub_second.shape[0]) // TILE
    tile_terms = jnp.einsum(
        "rtij,rid->rtjd",
        tile_vals,
        agg_grad.reshape(-1, TILE, D),
        preferred_element_type=jnp.float32,
    )
    selector = (
        tile_cols[:, :, None] == jnp.arange(source_tiles, dtype=jnp.int32)[None, None, :]
    ).astype(jnp.float32)
    spread = jnp.einsum(
        "rts,rtjd->sjd", selector, tile_terms, precision=lax.Precision.HIGHEST
    ).reshape(-1, D)
    own_grad = spread[:V_DEV]
    hub_grad = lax.psum_scatter(spread[V_DEV + HALO :], "group", scatter_dimension=0, tiled=True)
    vertex_grad = own_grad.at[owned_hubs].add(hub_grad)
    gate_value = jax.nn.sigmoid(z_first)
    dz_first = (vertex_grad * gate_value * (1.0 + z_first * (1.0 - gate_value))).astype(
        jnp.bfloat16
    )
    grad_first = reduce_weight(dz_first, agg_first)
    return (new_history, vertex_grad.astype(jnp.bfloat16), grad_first, grad_second)


BF16, F32 = jnp.bfloat16, jnp.float32


def dot(left, right, contract=(1, 0)):
    dims = (((contract[0],), (contract[1],)), ((), ()))
    return lax.dot_general(left, right, dims, preferred_element_type=F32)


def halves(weights):
    high = weights.astype(BF16)
    low = (weights - high.astype(F32)).astype(BF16)
    return jnp.concatenate([high, low], axis=0)


def apply_halves(pair, rows):
    both = dot(pair, rows)
    count = pair.shape[0] // 2
    return both[:count] + both[count:]


def window_kernel(
    groups,
    doms,
    feats_given,
    history_given,
    grad_given,
    w_first,
    w_second,
    send_given,
    halo_given,
    hubs_given,
    cols_given,
    vals_given,
    new_history,
    embed_grad,
    grad_first,
    grad_second,
    w_first_held,
    w_second_held,
    feats,
    history,
    send_index,
    halo_index,
    hub_rows,
    tile_cols,
    tile_vals,
    send_feats,
    send_hist,
    send_hubs,
    send_fresh,
    slots_feats,
    slots_hist,
    hubs_first,
    hubs_second,
    all_grad_out,
    all_agg,
    hub_terms,
    hub_arrived,
    own_grad,
    gate_slope,
    dz_out,
    dz_in,
    agg_out,
    agg_in,
    first_terms,
    first_sent,
    first_in,
    second_terms,
    second_sent,
    second_in,
    rows_out,
    rows_in,
    local_sems,
    send_sems,
    recv_sems,
):
    group, dom = lax.axis_index("group"), lax.axis_index("dom")
    chip, core = dom // 2, dom % 2
    factor = 1.0 / math.sqrt(V_DEV * groups * doms)
    share = D // (groups * doms)
    dom_peers = [(dom + off) % doms for off in range(1, doms)]
    group_peers = [(group + off) % groups for off in range(1, groups)]
    sibling = dom + 1 - 2 * core
    beside = (chip + 1 - 2 * (chip % 2)) * 2 + core
    across = ((chip + 2) % 4) * 2 + core
    opposite = (3 - chip) * 2 + core
    used = []

    barrier = pltpu.get_barrier_semaphore()
    for peer in dom_peers:
        pl.semaphore_signal(
            barrier, inc=1, device_id=(group, peer), device_id_type=pl.DeviceIdType.MESH
        )
    for peer in group_peers:
        pl.semaphore_signal(
            barrier, inc=1, device_id=(peer, dom), device_id_type=pl.DeviceIdType.MESH
        )

    loads = []
    for source, target in (
        (send_given, send_index),
        (hubs_given, hub_rows),
        (feats_given, feats),
        (history_given, history),
        (grad_given, all_grad_out.at[dom]),
        (halo_given, halo_index),
        (cols_given, tile_cols),
        (vals_given, tile_vals),
        (w_second, w_second_held),
        (w_first, w_first_held),
    ):
        loads.append(pltpu.make_async_copy(source, target, local_sems.at[len(loads)]))
        loads[-1].start()

    def send(source, target, to_group, to_dom):
        copy = pltpu.make_async_remote_copy(
            src_ref=source,
            dst_ref=target,
            send_sem=send_sems.at[len(used)],
            recv_sem=recv_sems.at[len(used)],
            device_id=(to_group, to_dom),
            device_id_type=pl.DeviceIdType.MESH,
        )
        used.append(copy)
        copy.start()
        return copy

    def to_doms(source, target):
        return [send(source.at[peer], target.at[dom], group, peer) for peer in dom_peers]

    def to_groups(source, target):
        return [send(source.at[peer], target.at[group], peer, dom) for peer in group_peers]

    def share_to_groups(source, target):
        return [send(source, target.at[group], peer, dom) for peer in group_peers]

    def to_near(target):
        block = target.at[dom]
        return [send(block, block, group, peer) for peer in (sibling, beside, across)]

    def relay(near, target):
        near[1].wait_recv()
        block = target.at[beside]
        upper = target.at[beside, pl.ds(0, V_DEV // 2)]
        parts = [send(upper, upper, group, across)]
        passed = [send(block, block, group, sibling)]
        near[2].wait_recv()
        block = target.at[across]
        lower = target.at[across, pl.ds(V_DEV // 2, V_DEV // 2)]
        parts.append(send(lower, lower, group, beside))
        passed.append(send(block, block, group, sibling))
        return parts, passed

    def finish(near, parts, passed, target):
        arrived(parts)
        block = target.at[opposite]
        arrived([near[0]] + passed + [send(block, block, group, sibling)])

    def arrived(copies):
        for copy in copies:
            copy.wait_recv()

    lane_row = lax.broadcasted_iota(jnp.int32, (1, V_DEV), 1)
    cap, hub_count = send_index.shape[2], hub_rows.shape[1]
    loads[0].wait()
    routes = jnp.broadcast_to(
        send_index[0].astype(F32)[:, None, :], (doms, cap, cap)
    ).reshape(doms * cap, cap)
    at_lane = lax.broadcasted_iota(jnp.int32, (doms * cap, cap), 1)
    at_slot = lax.broadcasted_iota(jnp.int32, (doms * cap, cap), 0) % cap
    route_column = jnp.sum(jnp.where(at_lane == at_slot, routes, 0.0), axis=1, keepdims=True)
    route_pick = (lane_row.astype(F32) == route_column).astype(F32).astype(BF16)
    loads[1].wait()
    hub_square = jnp.broadcast_to(hub_rows[...].astype(F32), (hub_count, hub_count))
    diagonal = lax.broadcasted_iota(jnp.int32, (hub_count, hub_count), 0) == (
        lax.broadcasted_iota(jnp.int32, (hub_count, hub_count), 1)
    )
    hub_column = jnp.sum(jnp.where(diagonal, hub_square, 0.0), axis=1, keepdims=True)
    hub_chosen = (lane_row.astype(F32) == hub_column).astype(F32)
    hub_pick = hub_chosen.astype(BF16)
    hub_spread = jnp.concatenate([hub_chosen] * groups, axis=0).T.astype(BF16)
    loads[2].wait()

    send_hubs[...] = dot(hub_pick, feats[...]).astype(BF16)
    pl.semaphore_wait(barrier, doms - 1 + groups - 1)
    hub_copies = share_to_groups(send_hubs, hubs_first)
    send_feats[...] = dot(route_pick, feats[...]).astype(BF16).reshape(send_feats.shape)
    feat_copies = to_doms(send_feats, slots_feats)
    loads[4].wait()
    grad_near = to_near(all_grad_out)
    slots_feats[dom] = send_feats[dom]
    hubs_first[group] = send_hubs[...]
    loads[3].wait()
    send_hist[...] = dot(route_pick, history[...]).astype(BF16).reshape(send_hist.shape)
    hist_copies = to_doms(send_hist, slots_hist)
    slots_hist[dom] = send_hist[dom]

    places = 3 * V_DEV
    place_of = lax.broadcasted_iota(jnp.int32, (places, V_DEV), 0)
    weights = jnp.zeros((V_DEV, places), F32)
    halo_tiles = HALO // TILE
    for load in loads[5:8]:
        load.wait()
    for tile in range(tile_vals.shape[1]):
        column = tile_cols[0:1, tile : tile + 1]
        target = jnp.where(column == 0, lane_row, lane_row + 2 * V_DEV)
        for halo in range(halo_tiles):
            slot = halo_index[halo * TILE : (halo + 1) * TILE].reshape(1, TILE) + V_DEV
            target = jnp.where(column == halo + 1, slot, target)
        chosen = (place_of == target).astype(F32).astype(BF16)
        weights = weights + dot(tile_vals[0, tile], chosen, (1, 1))
    own, slot, hub = (weights[:, n * V_DEV : (n + 1) * V_DEV] for n in range(3))
    own_pair, slot_pair, hub_pair = halves(own), halves(slot), halves(hub)

    loads[8].wait()
    agg_grad = dot(all_grad_out[dom], w_second_held[...], (1, 1)).astype(BF16)
    hub_terms[...] = apply_halves(halves(hub.T), agg_grad).astype(BF16).reshape(hub_terms.shape)
    term_copies = to_groups(hub_terms, hub_arrived)
    hub_arrived[group] = hub_terms[group]
    own_grad[...] = apply_halves(halves(own.T), agg_grad)

    first = apply_halves(own_pair, feats[...])
    arrived(feat_copies)
    first = first + apply_halves(slot_pair, slots_feats[...].reshape(V_DEV, D))
    arrived(hub_copies)
    first = first + apply_halves(hub_pair, hubs_first[...].reshape(V_DEV, D))
    agg_first = first.astype(BF16)
    all_agg[dom] = agg_first
    agg_near = to_near(all_agg)

    loads[9].wait()
    z_first = dot(agg_first, w_first_held[...])
    gate = 1.0 / (1.0 + jnp.exp(-z_first))
    fresh = (z_first * gate).astype(BF16)
    new_history[...] = fresh
    send_fresh[...] = dot(hub_pick, fresh).astype(BF16)
    fresh_copies = share_to_groups(send_fresh, hubs_second)
    hubs_second[group] = send_fresh[...]
    gate_slope[...] = gate * (1.0 + z_first * (1.0 - gate))

    arrived(term_copies)
    vertex_grad = own_grad[...] + dot(hub_spread, hub_arrived[...].reshape(V_DEV, D))
    embed_grad[...] = vertex_grad.astype(BF16)
    own_grad[...] = vertex_grad * gate_slope[...]
    for g in range(groups):
        for d in range(0, doms * share, TILE):
            start = g * doms * share + d
            block = own_grad[:, start : start + TILE].T.astype(BF16)
            for piece in range(TILE // share):
                dz_out[d // share + piece, g * share : (g + 1) * share, :] = block[
                    piece * share : (piece + 1) * share
                ]
    dz_copies = to_doms(dz_out, dz_in)
    dz_in[dom] = dz_out[dom]
    grad_parts, grad_passed = relay(grad_near, all_grad_out)

    arrived(hist_copies)
    second = apply_halves(own_pair, new_history[...])
    second = second + apply_halves(slot_pair, slots_hist[...].reshape(V_DEV, D))
    arrived(fresh_copies)
    second = second + apply_halves(hub_pair, hubs_second[...].reshape(V_DEV, D))
    wide = D // doms
    for d in range(doms):
        agg_out[d] = second[:, d * wide : (d + 1) * wide].T.astype(BF16)
    agg_copies = to_doms(agg_out, agg_in)
    agg_in[dom] = agg_out[dom]

    finish(grad_near, grad_parts, grad_passed, all_grad_out)
    agg_parts, agg_passed = relay(agg_near, all_agg)
    arrived(agg_copies)
    blocks = jnp.concatenate([agg_in[d] for d in range(doms)], axis=1)
    total = dot(blocks, all_grad_out[...].reshape(doms * V_DEV, D))
    per_group = D // groups
    for g in range(groups):
        for n in range(0, per_group, TILE):
            start = g * per_group + n
            block = total[:, start : start + TILE].T
            second_terms[g, n : n + TILE, :] = block
            second_sent[g, n : n + TILE, :] = block.astype(BF16)
    second_copies = to_groups(second_sent, second_in)

    finish(agg_near, agg_parts, agg_passed, all_agg)
    arrived(dz_copies)
    blocks = jnp.concatenate([dz_in[d] for d in range(doms)], axis=1)
    total = dot(blocks, all_agg[...].reshape(doms * V_DEV, D))
    first_terms[...] = total.reshape(first_terms.shape)
    first_sent[...] = total.astype(BF16).reshape(first_sent.shape)
    first_copies = to_groups(first_sent, first_in)

    arrived(second_copies)
    second_in[group] = jnp.zeros(second_in.shape[1:], BF16)
    total = second_terms[group]
    for g in range(groups):
        total = total + second_in[g].astype(F32)
    rows_out[...] = (total * factor).reshape(rows_out.shape)
    row_copies = to_doms(rows_out, rows_in)
    rows_in[dom] = rows_out[dom]

    arrived(first_copies)
    first_in[group] = jnp.zeros(first_in.shape[1:], BF16)
    total = first_terms[group]
    for g in range(groups):
        total = total + first_in[g].astype(F32)
    grad_first[...] = total * factor

    arrived(row_copies)
    for d in range(doms):
        grad_second[:, d * wide : (d + 1) * wide] = rows_in[d]
    for copy in used:
        copy.wait_send()


def write_kernel(*refs):
    given, written, staged, sems = refs[:4], refs[4:8], refs[8:12], refs[12]
    reads = [pltpu.make_async_copy(given[n], staged[n], sems.at[n]) for n in range(4)]
    writes = [pltpu.make_async_copy(staged[n], written[n], sems.at[n + 4]) for n in range(4)]
    for copy in reads:
        copy.start()
    for read, write in zip(reads, writes):
        read.wait()
        write.start()
    for copy in writes:
        copy.wait()


def in_kernel(
    feats, history, grad_out, w_first, w_second, send_index, halo_index, hub_rows, tile_cols, tile_vals
):
    groups, doms = lax.axis_size("group"), lax.axis_size("dom")
    share = D // (groups * doms)
    cap, hubs = send_index.shape[2], hub_rows.shape[1]
    wide, per_group = D // doms, D // groups
    copies = 5 * (doms - 1) + 5 * (groups - 1) + 16
    vmem = pl.BlockSpec(memory_space=pltpu.VMEM)
    hbm = pl.BlockSpec(memory_space=pltpu.HBM)
    held = pltpu.VMEM
    results = pl.pallas_call(
        functools.partial(window_kernel, groups, doms),
        out_shape=(
            jax.ShapeDtypeStruct((V_DEV, D), BF16),
            jax.ShapeDtypeStruct((V_DEV, D), BF16),
            jax.ShapeDtypeStruct((share, D), F32),
            jax.ShapeDtypeStruct((share, D), F32),
        ),
        in_specs=[hbm] * 10,
        out_specs=(vmem,) * 4,
        scratch_shapes=[
            held((D, D), BF16),
            held((D, D), BF16),
            held((V_DEV, D), BF16),
            held((V_DEV, D), BF16),
            held(send_index.shape, jnp.int32),
            held(halo_index.shape, jnp.int32),
            held(hub_rows.shape, jnp.int32),
            held(tile_cols.shape, jnp.int32),
            held(tile_vals.shape, BF16),
            held((doms, cap, D), BF16),
            held((doms, cap, D), BF16),
            held((hubs, D), BF16),
            held((hubs, D), BF16),
            held((doms, cap, D), BF16),
            held((doms, cap, D), BF16),
            held((groups, hubs, D), BF16),
            held((groups, hubs, D), BF16),
            held((doms, V_DEV, D), BF16),
            held((doms, V_DEV, D), BF16),
            held((groups, hubs, D), BF16),
            held((groups, hubs, D), BF16),
            held((V_DEV, D), F32),
            held((V_DEV, D), F32),
            held((doms, groups * share, V_DEV), BF16),
            held((doms, groups * share, V_DEV), BF16),
            held((doms, wide, V_DEV), BF16),
            held((doms, wide, V_DEV), BF16),
            held((groups, share, D), F32),
            held((groups, share, D), BF16),
            held((groups, share, D), BF16),
            held((groups, per_group, wide), F32),
            held((groups, per_group, wide), BF16),
            held((groups, per_group, wide), BF16),
            held((doms, share, wide), F32),
            held((doms, share, wide), F32),
            pltpu.SemaphoreType.DMA((10,)),
            pltpu.SemaphoreType.DMA((copies,)),
            pltpu.SemaphoreType.DMA((copies,)),
        ],
        compiler_params=pltpu.CompilerParams(
            collective_id=0, has_side_effects=True, vmem_limit_bytes=60 * 1024 * 1024
        ),
    )(
        feats,
        history,
        grad_out,
        w_first,
        w_second,
        send_index,
        halo_index,
        hub_rows,
        tile_cols,
        tile_vals,
    )
    shapes = [(part.shape, part.dtype) for part in results]
    return pl.pallas_call(
        write_kernel,
        out_shape=tuple(jax.ShapeDtypeStruct(*shape) for shape in shapes),
        in_specs=[pl.BlockSpec(memory_space=pl.ANY)] * 4,
        out_specs=(hbm,) * 4,
        scratch_shapes=[held(*shape) for shape in shapes] + [pltpu.SemaphoreType.DMA((8,))],
        compiler_params=pltpu.CompilerParams(vmem_limit_bytes=60 * 1024 * 1024),
    )(*results)


def fits_kernel(groups, doms, cap, hubs):
    return (
        D % (groups * doms * 16) == 0
        and TILE % (D // (groups * doms)) == 0
        and doms == 8
        and D // doms == V_DEV
        and doms * cap == V_DEV
        and groups * hubs == V_DEV
    )


def window(*args):
    send_index, hub_rows = args[5], args[7]
    groups, doms = lax.axis_size("group"), lax.axis_size("dom")
    if fits_kernel(groups, doms, send_index.shape[2], hub_rows.shape[1]):
        return in_kernel(*args)
    return on_device(*args)


def solution(mesh):
    placed = (
        P(("group", "dom"), None),
        P(("group", "dom"), None),
        P(("group", "dom"), None),
        P(),
        P(),
        P(("group", "dom"), None, None),
        P(("group", "dom")),
        P(("group", "dom"), None),
        P(("group", "dom"), None),
        P(("group", "dom"), None, None, None),
    )
    return jax.shard_map(
        window,
        mesh=mesh,
        in_specs=placed,
        out_specs=(
            P(("group", "dom"), None),
            P(("group", "dom"), None),
            P(("group", "dom"), None),
            P(("group", "dom"), None),
        ),
        check_vma=False,
    )
```

```python
import functools
import math

import jax
import jax.numpy as jnp
from jax import lax
from jax.experimental import pallas as pl
from jax.experimental.pallas import tpu as pltpu
from jax.sharding import PartitionSpec as P

D = 1024
V_DEV = 128
TILE = 128
HALO = 512


def combine_tiles(own_rows, halo_rows, hub_panel, tile_cols, tile_vals):
    source = jnp.concatenate([own_rows, halo_rows, hub_panel], axis=0)
    feature_width = source.shape[1]
    picked = source.reshape(-1, tile_vals.shape[2], feature_width)[tile_cols]
    summed = jnp.einsum("rtij,rtjd->rid", tile_vals, picked, preferred_element_type=jnp.float32)
    return summed.reshape(-1, feature_width).astype(jnp.bfloat16)


def reduce_weight(left_rows, right_rows):
    groups, doms = lax.axis_size("group"), lax.axis_size("dom")
    factor = 1.0 / math.sqrt(left_rows.shape[0] * groups * doms)
    rows = left_rows.shape[0]
    gathered = lax.all_gather(right_rows, "dom", axis=0, tiled=True)
    by_dom = left_rows.reshape(rows, groups, doms, -1).transpose(2, 0, 1, 3).reshape(doms * rows, -1)
    columns = lax.all_to_all(by_dom, "dom", split_axis=0, concat_axis=0, tiled=True)
    product = lax.dot_general(
        columns, gathered, (((0,), (0,)), ((), ())), preferred_element_type=jnp.float32
    )
    summed = lax.psum_scatter(product, "group", scatter_dimension=0, tiled=True)
    return summed * factor


def on_device(
    feats,
    history,
    grad_out,
    w_first,
    w_second,
    send_index,
    halo_index,
    hub_rows,
    tile_cols,
    tile_vals,
):
    routes = send_index[0]
    owned_hubs = hub_rows[0]
    feat_slots = lax.all_to_all(feats[routes], "dom", split_axis=0, concat_axis=0, tiled=True)
    feat_halo = feat_slots.reshape(-1, D)[halo_index]
    hub_first = lax.all_gather(feats[owned_hubs], "group", axis=0, tiled=True)
    agg_first = combine_tiles(feats, feat_halo, hub_first, tile_cols, tile_vals)
    z_first = jnp.dot(agg_first, w_first, preferred_element_type=jnp.float32)
    new_history = jax.nn.silu(z_first).astype(jnp.bfloat16)
    hist_slots = lax.all_to_all(history[routes], "dom", split_axis=0, concat_axis=0, tiled=True)
    hist_halo = hist_slots.reshape(-1, D)[halo_index]
    hub_second = lax.all_gather(new_history[owned_hubs], "group", axis=0, tiled=True)
    agg_second = combine_tiles(new_history, hist_halo, hub_second, tile_cols, tile_vals)
    grad_second = reduce_weight(grad_out, agg_second)
    agg_grad = lax.dot_general(
        grad_out, w_second, (((1,), (1,)), ((), ())), preferred_element_type=jnp.float32
    ).astype(jnp.bfloat16)
    source_tiles = (V_DEV + HALO + hub_second.shape[0]) // TILE
    tile_terms = jnp.einsum(
        "rtij,rid->rtjd",
        tile_vals,
        agg_grad.reshape(-1, TILE, D),
        preferred_element_type=jnp.float32,
    )
    selector = (
        tile_cols[:, :, None] == jnp.arange(source_tiles, dtype=jnp.int32)[None, None, :]
    ).astype(jnp.float32)
    spread = jnp.einsum(
        "rts,rtjd->sjd", selector, tile_terms, precision=lax.Precision.HIGHEST
    ).reshape(-1, D)
    own_grad = spread[:V_DEV]
    hub_grad = lax.psum_scatter(spread[V_DEV + HALO :], "group", scatter_dimension=0, tiled=True)
    vertex_grad = own_grad.at[owned_hubs].add(hub_grad)
    gate_value = jax.nn.sigmoid(z_first)
    dz_first = (vertex_grad * gate_value * (1.0 + z_first * (1.0 - gate_value))).astype(
        jnp.bfloat16
    )
    grad_first = reduce_weight(dz_first, agg_first)
    return (new_history, vertex_grad.astype(jnp.bfloat16), grad_first, grad_second)


BF16, F32 = jnp.bfloat16, jnp.float32


def dot(left, right, contract=(1, 0)):
    dims = (((contract[0],), (contract[1],)), ((), ()))
    return lax.dot_general(left, right, dims, preferred_element_type=F32)


def halves(weights):
    high = weights.astype(BF16)
    low = (weights - high.astype(F32)).astype(BF16)
    return jnp.concatenate([high, low], axis=0)


def apply_halves(pair, rows):
    both = dot(pair, rows)
    count = pair.shape[0] // 2
    return both[:count] + both[count:]


def window_kernel(
    groups,
    doms,
    feats_given,
    history_given,
    grad_given,
    w_first,
    w_second,
    send_given,
    halo_given,
    hubs_given,
    cols_given,
    vals_given,
    new_history,
    embed_grad,
    grad_first,
    grad_second,
    w_first_held,
    w_second_held,
    feats,
    history,
    send_index,
    halo_index,
    hub_rows,
    tile_cols,
    tile_vals,
    send_feats,
    send_hist,
    send_hubs,
    send_fresh,
    slots_feats,
    slots_hist,
    hubs_first,
    hubs_second,
    all_grad_out,
    all_agg,
    hub_terms,
    hub_arrived,
    own_grad,
    gate_slope,
    dz_out,
    dz_in,
    agg_out,
    agg_in,
    first_terms,
    first_sent,
    first_in,
    second_terms,
    second_sent,
    second_in,
    rows_out,
    rows_in,
    local_sems,
    send_sems,
    recv_sems,
):
    group, dom = lax.axis_index("group"), lax.axis_index("dom")
    chip, core = dom // 2, dom % 2
    factor = 1.0 / math.sqrt(V_DEV * groups * doms)
    share = D // (groups * doms)
    dom_peers = [(dom + off) % doms for off in range(1, doms)]
    group_peers = [(group + off) % groups for off in range(1, groups)]
    sibling = dom + 1 - 2 * core
    beside = (chip + 1 - 2 * (chip % 2)) * 2 + core
    across = ((chip + 2) % 4) * 2 + core
    opposite = (3 - chip) * 2 + core
    used = []

    barrier = pltpu.get_barrier_semaphore()
    for peer in dom_peers:
        pl.semaphore_signal(
            barrier, inc=1, device_id=(group, peer), device_id_type=pl.DeviceIdType.MESH
        )
    for peer in group_peers:
        pl.semaphore_signal(
            barrier, inc=1, device_id=(peer, dom), device_id_type=pl.DeviceIdType.MESH
        )

    loads = []
    for source, target in (
        (send_given, send_index),
        (hubs_given, hub_rows),
        (feats_given, feats),
        (history_given, history),
        (grad_given, all_grad_out.at[dom]),
        (halo_given, halo_index),
        (cols_given, tile_cols),
        (vals_given, tile_vals),
        (w_second, w_second_held),
        (w_first, w_first_held),
    ):
        loads.append(pltpu.make_async_copy(source, target, local_sems.at[len(loads)]))
        loads[-1].start()

    def send(source, target, to_group, to_dom):
        copy = pltpu.make_async_remote_copy(
            src_ref=source,
            dst_ref=target,
            send_sem=send_sems.at[len(used)],
            recv_sem=recv_sems.at[len(used)],
            device_id=(to_group, to_dom),
            device_id_type=pl.DeviceIdType.MESH,
        )
        used.append(copy)
        copy.start()
        return copy

    def to_doms(source, target):
        return [send(source.at[peer], target.at[dom], group, peer) for peer in dom_peers]

    def to_groups(source, target):
        return [send(source.at[peer], target.at[group], peer, dom) for peer in group_peers]

    def share_to_groups(source, target):
        return [send(source, target.at[group], peer, dom) for peer in group_peers]

    def to_near(target):
        block = target.at[dom]
        return [send(block, block, group, peer) for peer in (sibling, beside, across)]

    def relay(near, target):
        near[1].wait_recv()
        block = target.at[beside]
        upper = target.at[beside, pl.ds(0, V_DEV // 2)]
        parts = [send(upper, upper, group, across)]
        passed = [send(block, block, group, sibling)]
        near[2].wait_recv()
        block = target.at[across]
        lower = target.at[across, pl.ds(V_DEV // 2, V_DEV // 2)]
        parts.append(send(lower, lower, group, beside))
        passed.append(send(block, block, group, sibling))
        return parts, passed

    def finish(near, parts, passed, target):
        arrived(parts)
        block = target.at[opposite]
        arrived([near[0]] + passed + [send(block, block, group, sibling)])

    def arrived(copies):
        for copy in copies:
            copy.wait_recv()

    lane_row = lax.broadcasted_iota(jnp.int32, (1, V_DEV), 1)
    cap, hub_count = send_index.shape[2], hub_rows.shape[1]
    loads[0].wait()
    routes = jnp.broadcast_to(
        send_index[0].astype(F32)[:, None, :], (doms, cap, cap)
    ).reshape(doms * cap, cap)
    at_lane = lax.broadcasted_iota(jnp.int32, (doms * cap, cap), 1)
    at_slot = lax.broadcasted_iota(jnp.int32, (doms * cap, cap), 0) % cap
    route_column = jnp.sum(jnp.where(at_lane == at_slot, routes, 0.0), axis=1, keepdims=True)
    route_pick = (lane_row.astype(F32) == route_column).astype(F32).astype(BF16)
    loads[1].wait()
    hub_square = jnp.broadcast_to(hub_rows[...].astype(F32), (hub_count, hub_count))
    diagonal = lax.broadcasted_iota(jnp.int32, (hub_count, hub_count), 0) == (
        lax.broadcasted_iota(jnp.int32, (hub_count, hub_count), 1)
    )
    hub_column = jnp.sum(jnp.where(diagonal, hub_square, 0.0), axis=1, keepdims=True)
    hub_chosen = (lane_row.astype(F32) == hub_column).astype(F32)
    hub_pick = hub_chosen.astype(BF16)
    hub_spread = jnp.concatenate([hub_chosen] * groups, axis=0).T.astype(BF16)
    loads[2].wait()

    send_hubs[...] = dot(hub_pick, feats[...]).astype(BF16)
    pl.semaphore_wait(barrier, doms - 1 + groups - 1)
    hub_copies = share_to_groups(send_hubs, hubs_first)
    send_feats[...] = dot(route_pick, feats[...]).astype(BF16).reshape(send_feats.shape)
    feat_copies = to_doms(send_feats, slots_feats)
    loads[4].wait()
    grad_near = to_near(all_grad_out)
    slots_feats[dom] = send_feats[dom]
    hubs_first[group] = send_hubs[...]
    loads[3].wait()
    send_hist[...] = dot(route_pick, history[...]).astype(BF16).reshape(send_hist.shape)
    hist_copies = to_doms(send_hist, slots_hist)
    slots_hist[dom] = send_hist[dom]

    places = 3 * V_DEV
    place_of = lax.broadcasted_iota(jnp.int32, (places, V_DEV), 0)
    weights = jnp.zeros((V_DEV, places), F32)
    halo_tiles = HALO // TILE
    for load in loads[5:8]:
        load.wait()
    for tile in range(tile_vals.shape[1]):
        column = tile_cols[0:1, tile : tile + 1]
        target = jnp.where(column == 0, lane_row, lane_row + 2 * V_DEV)
        for halo in range(halo_tiles):
            slot = halo_index[halo * TILE : (halo + 1) * TILE].reshape(1, TILE) + V_DEV
            target = jnp.where(column == halo + 1, slot, target)
        chosen = (place_of == target).astype(F32).astype(BF16)
        weights = weights + dot(tile_vals[0, tile], chosen, (1, 1))
    own, slot, hub = (weights[:, n * V_DEV : (n + 1) * V_DEV] for n in range(3))
    own_pair, slot_pair, hub_pair = halves(own), halves(slot), halves(hub)

    loads[8].wait()
    agg_grad = dot(all_grad_out[dom], w_second_held[...], (1, 1)).astype(BF16)
    hub_terms[...] = apply_halves(halves(hub.T), agg_grad).astype(BF16).reshape(hub_terms.shape)
    term_copies = to_groups(hub_terms, hub_arrived)
    hub_arrived[group] = hub_terms[group]
    own_grad[...] = apply_halves(halves(own.T), agg_grad)

    first = apply_halves(own_pair, feats[...])
    arrived(feat_copies)
    first = first + apply_halves(slot_pair, slots_feats[...].reshape(V_DEV, D))
    arrived(hub_copies)
    first = first + apply_halves(hub_pair, hubs_first[...].reshape(V_DEV, D))
    agg_first = first.astype(BF16)
    all_agg[dom] = agg_first
    agg_near = to_near(all_agg)

    loads[9].wait()
    z_first = dot(agg_first, w_first_held[...])
    gate = 1.0 / (1.0 + jnp.exp(-z_first))
    fresh = (z_first * gate).astype(BF16)
    new_history[...] = fresh
    send_fresh[...] = dot(hub_pick, fresh).astype(BF16)
    fresh_copies = share_to_groups(send_fresh, hubs_second)
    hubs_second[group] = send_fresh[...]
    gate_slope[...] = gate * (1.0 + z_first * (1.0 - gate))
    grad_parts, grad_passed = relay(grad_near, all_grad_out)

    arrived(term_copies)
    vertex_grad = own_grad[...] + dot(hub_spread, hub_arrived[...].reshape(V_DEV, D))
    embed_grad[...] = vertex_grad.astype(BF16)
    own_grad[...] = vertex_grad * gate_slope[...]
    for g in range(groups):
        for d in range(0, doms * share, TILE):
            start = g * doms * share + d
            block = own_grad[:, start : start + TILE].T.astype(BF16)
            for piece in range(TILE // share):
                dz_out[d // share + piece, g * share : (g + 1) * share, :] = block[
                    piece * share : (piece + 1) * share
                ]
    dz_copies = to_doms(dz_out, dz_in)
    dz_in[dom] = dz_out[dom]

    arrived(hist_copies)
    second = apply_halves(own_pair, new_history[...])
    second = second + apply_halves(slot_pair, slots_hist[...].reshape(V_DEV, D))
    agg_parts, agg_passed = relay(agg_near, all_agg)
    arrived(fresh_copies)
    second = second + apply_halves(hub_pair, hubs_second[...].reshape(V_DEV, D))
    wide = D // doms
    for d in range(doms):
        agg_out[d] = second[:, d * wide : (d + 1) * wide].T.astype(BF16)
    agg_copies = to_doms(agg_out, agg_in)
    agg_in[dom] = agg_out[dom]

    finish(grad_near, grad_parts, grad_passed, all_grad_out)
    arrived(agg_copies)
    blocks = jnp.concatenate([agg_in[d] for d in range(doms)], axis=1)
    total = dot(blocks, all_grad_out[...].reshape(doms * V_DEV, D))
    per_group = D // groups
    for g in range(groups):
        for n in range(0, per_group, TILE):
            start = g * per_group + n
            block = total[:, start : start + TILE].T
            second_terms[g, n : n + TILE, :] = block
            second_sent[g, n : n + TILE, :] = block.astype(BF16)
    second_copies = to_groups(second_sent, second_in)

    finish(agg_near, agg_parts, agg_passed, all_agg)
    arrived(dz_copies)
    blocks = jnp.concatenate([dz_in[d] for d in range(doms)], axis=1)
    total = dot(blocks, all_agg[...].reshape(doms * V_DEV, D))
    first_terms[...] = total.reshape(first_terms.shape)
    first_sent[...] = total.astype(BF16).reshape(first_sent.shape)
    first_copies = to_groups(first_sent, first_in)

    arrived(second_copies)
    second_in[group] = jnp.zeros(second_in.shape[1:], BF16)
    total = second_terms[group]
    for g in range(groups):
        total = total + second_in[g].astype(F32)
    rows_out[...] = (total * factor).reshape(rows_out.shape)
    row_copies = to_doms(rows_out, rows_in)
    rows_in[dom] = rows_out[dom]

    arrived(first_copies)
    first_in[group] = jnp.zeros(first_in.shape[1:], BF16)
    total = first_terms[group]
    for g in range(groups):
        total = total + first_in[g].astype(F32)
    grad_first[...] = total * factor

    arrived(row_copies)
    for d in range(doms):
        grad_second[:, d * wide : (d + 1) * wide] = rows_in[d]
    for copy in used:
        copy.wait_send()


def write_kernel(*refs):
    given, written, staged, sems = refs[:4], refs[4:8], refs[8:12], refs[12]
    reads = [pltpu.make_async_copy(given[n], staged[n], sems.at[n]) for n in range(4)]
    writes = [pltpu.make_async_copy(staged[n], written[n], sems.at[n + 4]) for n in range(4)]
    for copy in reads:
        copy.start()
    for read, write in zip(reads, writes):
        read.wait()
        write.start()
    for copy in writes:
        copy.wait()


def in_kernel(
    feats, history, grad_out, w_first, w_second, send_index, halo_index, hub_rows, tile_cols, tile_vals
):
    groups, doms = lax.axis_size("group"), lax.axis_size("dom")
    share = D // (groups * doms)
    cap, hubs = send_index.shape[2], hub_rows.shape[1]
    wide, per_group = D // doms, D // groups
    copies = 5 * (doms - 1) + 5 * (groups - 1) + 16
    vmem = pl.BlockSpec(memory_space=pltpu.VMEM)
    hbm = pl.BlockSpec(memory_space=pltpu.HBM)
    held = pltpu.VMEM
    results = pl.pallas_call(
        functools.partial(window_kernel, groups, doms),
        out_shape=(
            jax.ShapeDtypeStruct((V_DEV, D), BF16),
            jax.ShapeDtypeStruct((V_DEV, D), BF16),
            jax.ShapeDtypeStruct((share, D), F32),
            jax.ShapeDtypeStruct((share, D), F32),
        ),
        in_specs=[hbm] * 10,
        out_specs=(vmem,) * 4,
        scratch_shapes=[
            held((D, D), BF16),
            held((D, D), BF16),
            held((V_DEV, D), BF16),
            held((V_DEV, D), BF16),
            held(send_index.shape, jnp.int32),
            held(halo_index.shape, jnp.int32),
            held(hub_rows.shape, jnp.int32),
            held(tile_cols.shape, jnp.int32),
            held(tile_vals.shape, BF16),
            held((doms, cap, D), BF16),
            held((doms, cap, D), BF16),
            held((hubs, D), BF16),
            held((hubs, D), BF16),
            held((doms, cap, D), BF16),
            held((doms, cap, D), BF16),
            held((groups, hubs, D), BF16),
            held((groups, hubs, D), BF16),
            held((doms, V_DEV, D), BF16),
            held((doms, V_DEV, D), BF16),
            held((groups, hubs, D), BF16),
            held((groups, hubs, D), BF16),
            held((V_DEV, D), F32),
            held((V_DEV, D), F32),
            held((doms, groups * share, V_DEV), BF16),
            held((doms, groups * share, V_DEV), BF16),
            held((doms, wide, V_DEV), BF16),
            held((doms, wide, V_DEV), BF16),
            held((groups, share, D), F32),
            held((groups, share, D), BF16),
            held((groups, share, D), BF16),
            held((groups, per_group, wide), F32),
            held((groups, per_group, wide), BF16),
            held((groups, per_group, wide), BF16),
            held((doms, share, wide), F32),
            held((doms, share, wide), F32),
            pltpu.SemaphoreType.DMA((10,)),
            pltpu.SemaphoreType.DMA((copies,)),
            pltpu.SemaphoreType.DMA((copies,)),
        ],
        compiler_params=pltpu.CompilerParams(
            collective_id=0, has_side_effects=True, vmem_limit_bytes=60 * 1024 * 1024
        ),
    )(
        feats,
        history,
        grad_out,
        w_first,
        w_second,
        send_index,
        halo_index,
        hub_rows,
        tile_cols,
        tile_vals,
    )
    shapes = [(part.shape, part.dtype) for part in results]
    return pl.pallas_call(
        write_kernel,
        out_shape=tuple(jax.ShapeDtypeStruct(*shape) for shape in shapes),
        in_specs=[pl.BlockSpec(memory_space=pl.ANY)] * 4,
        out_specs=(hbm,) * 4,
        scratch_shapes=[held(*shape) for shape in shapes] + [pltpu.SemaphoreType.DMA((8,))],
        compiler_params=pltpu.CompilerParams(vmem_limit_bytes=60 * 1024 * 1024),
    )(*results)


def fits_kernel(groups, doms, cap, hubs):
    return (
        D % (groups * doms * 16) == 0
        and TILE % (D // (groups * doms)) == 0
        and doms == 8
        and D // doms == V_DEV
        and doms * cap == V_DEV
        and groups * hubs == V_DEV
    )


def window(*args):
    send_index, hub_rows = args[5], args[7]
    groups, doms = lax.axis_size("group"), lax.axis_size("dom")
    if fits_kernel(groups, doms, send_index.shape[2], hub_rows.shape[1]):
        return in_kernel(*args)
    return on_device(*args)


def solution(mesh):
    placed = (
        P(("group", "dom"), None),
        P(("group", "dom"), None),
        P(("group", "dom"), None),
        P(),
        P(),
        P(("group", "dom"), None, None),
        P(("group", "dom")),
        P(("group", "dom"), None),
        P(("group", "dom"), None),
        P(("group", "dom"), None, None, None),
    )
    return jax.shard_map(
        window,
        mesh=mesh,
        in_specs=placed,
        out_specs=(
            P(("group", "dom"), None),
            P(("group", "dom"), None),
            P(("group", "dom"), None),
            P(("group", "dom"), None),
        ),
        check_vma=False,
    )
```

```python
import functools
import math

import jax
import jax.numpy as jnp
from jax import lax
from jax.experimental import pallas as pl
from jax.experimental.pallas import tpu as pltpu
from jax.sharding import PartitionSpec as P

D = 1024
V_DEV = 128
TILE = 128
HALO = 512


def combine_tiles(own_rows, halo_rows, hub_panel, tile_cols, tile_vals):
    source = jnp.concatenate([own_rows, halo_rows, hub_panel], axis=0)
    feature_width = source.shape[1]
    picked = source.reshape(-1, tile_vals.shape[2], feature_width)[tile_cols]
    summed = jnp.einsum("rtij,rtjd->rid", tile_vals, picked, preferred_element_type=jnp.float32)
    return summed.reshape(-1, feature_width).astype(jnp.bfloat16)


def reduce_weight(left_rows, right_rows):
    groups, doms = lax.axis_size("group"), lax.axis_size("dom")
    factor = 1.0 / math.sqrt(left_rows.shape[0] * groups * doms)
    rows = left_rows.shape[0]
    gathered = lax.all_gather(right_rows, "dom", axis=0, tiled=True)
    by_dom = left_rows.reshape(rows, groups, doms, -1).transpose(2, 0, 1, 3).reshape(doms * rows, -1)
    columns = lax.all_to_all(by_dom, "dom", split_axis=0, concat_axis=0, tiled=True)
    product = lax.dot_general(
        columns, gathered, (((0,), (0,)), ((), ())), preferred_element_type=jnp.float32
    )
    summed = lax.psum_scatter(product, "group", scatter_dimension=0, tiled=True)
    return summed * factor


def on_device(
    feats,
    history,
    grad_out,
    w_first,
    w_second,
    send_index,
    halo_index,
    hub_rows,
    tile_cols,
    tile_vals,
):
    routes = send_index[0]
    owned_hubs = hub_rows[0]
    feat_slots = lax.all_to_all(feats[routes], "dom", split_axis=0, concat_axis=0, tiled=True)
    feat_halo = feat_slots.reshape(-1, D)[halo_index]
    hub_first = lax.all_gather(feats[owned_hubs], "group", axis=0, tiled=True)
    agg_first = combine_tiles(feats, feat_halo, hub_first, tile_cols, tile_vals)
    z_first = jnp.dot(agg_first, w_first, preferred_element_type=jnp.float32)
    new_history = jax.nn.silu(z_first).astype(jnp.bfloat16)
    hist_slots = lax.all_to_all(history[routes], "dom", split_axis=0, concat_axis=0, tiled=True)
    hist_halo = hist_slots.reshape(-1, D)[halo_index]
    hub_second = lax.all_gather(new_history[owned_hubs], "group", axis=0, tiled=True)
    agg_second = combine_tiles(new_history, hist_halo, hub_second, tile_cols, tile_vals)
    grad_second = reduce_weight(grad_out, agg_second)
    agg_grad = lax.dot_general(
        grad_out, w_second, (((1,), (1,)), ((), ())), preferred_element_type=jnp.float32
    ).astype(jnp.bfloat16)
    source_tiles = (V_DEV + HALO + hub_second.shape[0]) // TILE
    tile_terms = jnp.einsum(
        "rtij,rid->rtjd",
        tile_vals,
        agg_grad.reshape(-1, TILE, D),
        preferred_element_type=jnp.float32,
    )
    selector = (
        tile_cols[:, :, None] == jnp.arange(source_tiles, dtype=jnp.int32)[None, None, :]
    ).astype(jnp.float32)
    spread = jnp.einsum(
        "rts,rtjd->sjd", selector, tile_terms, precision=lax.Precision.HIGHEST
    ).reshape(-1, D)
    own_grad = spread[:V_DEV]
    hub_grad = lax.psum_scatter(spread[V_DEV + HALO :], "group", scatter_dimension=0, tiled=True)
    vertex_grad = own_grad.at[owned_hubs].add(hub_grad)
    gate_value = jax.nn.sigmoid(z_first)
    dz_first = (vertex_grad * gate_value * (1.0 + z_first * (1.0 - gate_value))).astype(
        jnp.bfloat16
    )
    grad_first = reduce_weight(dz_first, agg_first)
    return (new_history, vertex_grad.astype(jnp.bfloat16), grad_first, grad_second)


BF16, F32 = jnp.bfloat16, jnp.float32


def dot(left, right, contract=(1, 0)):
    dims = (((contract[0],), (contract[1],)), ((), ()))
    return lax.dot_general(left, right, dims, preferred_element_type=F32)


def halves(weights):
    high = weights.astype(BF16)
    low = (weights - high.astype(F32)).astype(BF16)
    return jnp.concatenate([high, low], axis=0)


def apply_halves(pair, rows):
    both = dot(pair, rows)
    count = pair.shape[0] // 2
    return both[:count] + both[count:]


def window_kernel(
    groups,
    doms,
    feats_given,
    history_given,
    grad_given,
    w_first,
    w_second,
    send_given,
    halo_given,
    hubs_given,
    cols_given,
    vals_given,
    new_history,
    embed_grad,
    grad_first,
    grad_second,
    w_first_held,
    w_second_held,
    feats,
    history,
    send_index,
    halo_index,
    hub_rows,
    tile_cols,
    tile_vals,
    send_feats,
    send_hist,
    send_hubs,
    send_fresh,
    slots_feats,
    slots_hist,
    hubs_first,
    hubs_second,
    all_grad_out,
    all_agg,
    hub_terms,
    hub_arrived,
    own_grad,
    gate_slope,
    dz_out,
    dz_in,
    agg_out,
    agg_in,
    first_terms,
    first_sent,
    first_in,
    second_terms,
    second_sent,
    second_in,
    rows_out,
    rows_in,
    local_sems,
    send_sems,
    recv_sems,
):
    group, dom = lax.axis_index("group"), lax.axis_index("dom")
    chip, core = dom // 2, dom % 2
    factor = 1.0 / math.sqrt(V_DEV * groups * doms)
    share = D // (groups * doms)
    dom_peers = [(dom + off) % doms for off in range(1, doms)]
    group_peers = [(group + off) % groups for off in range(1, groups)]
    sibling = dom + 1 - 2 * core
    beside = (chip + 1 - 2 * (chip % 2)) * 2 + core
    across = ((chip + 2) % 4) * 2 + core
    opposite = (3 - chip) * 2 + core
    used = []

    barrier = pltpu.get_barrier_semaphore()
    for peer in dom_peers:
        pl.semaphore_signal(
            barrier, inc=1, device_id=(group, peer), device_id_type=pl.DeviceIdType.MESH
        )
    for peer in group_peers:
        pl.semaphore_signal(
            barrier, inc=1, device_id=(peer, dom), device_id_type=pl.DeviceIdType.MESH
        )

    loads = []
    for source, target in (
        (send_given, send_index),
        (hubs_given, hub_rows),
        (feats_given, feats),
        (history_given, history),
        (grad_given, all_grad_out.at[dom]),
        (halo_given, halo_index),
        (cols_given, tile_cols),
        (vals_given, tile_vals),
        (w_second, w_second_held),
        (w_first, w_first_held),
    ):
        loads.append(pltpu.make_async_copy(source, target, local_sems.at[len(loads)]))
        loads[-1].start()

    def send(source, target, to_group, to_dom):
        copy = pltpu.make_async_remote_copy(
            src_ref=source,
            dst_ref=target,
            send_sem=send_sems.at[len(used)],
            recv_sem=recv_sems.at[len(used)],
            device_id=(to_group, to_dom),
            device_id_type=pl.DeviceIdType.MESH,
        )
        used.append(copy)
        copy.start()
        return copy

    def to_doms(source, target):
        return [send(source.at[peer], target.at[dom], group, peer) for peer in dom_peers]

    def to_groups(source, target):
        return [send(source.at[peer], target.at[group], peer, dom) for peer in group_peers]

    def share_to_groups(source, target):
        return [send(source, target.at[group], peer, dom) for peer in group_peers]

    def to_near(target):
        block = target.at[dom]
        return [send(block, block, group, peer) for peer in (sibling, beside, across)]

    def relay(near, target):
        near[1].wait_recv()
        block = target.at[beside]
        upper = target.at[beside, pl.ds(0, V_DEV // 2)]
        parts = [send(upper, upper, group, across)]
        passed = [send(block, block, group, sibling)]
        near[2].wait_recv()
        block = target.at[across]
        lower = target.at[across, pl.ds(V_DEV // 2, V_DEV // 2)]
        parts.append(send(lower, lower, group, beside))
        passed.append(send(block, block, group, sibling))
        return parts, passed

    def finish(near, parts, passed, target):
        arrived(parts)
        block = target.at[opposite]
        arrived([near[0]] + passed + [send(block, block, group, sibling)])

    def arrived(copies):
        for copy in copies:
            copy.wait_recv()

    lane_row = lax.broadcasted_iota(jnp.int32, (1, V_DEV), 1)
    cap, hub_count = send_index.shape[2], hub_rows.shape[1]
    loads[0].wait()
    routes = jnp.broadcast_to(
        send_index[0].astype(F32)[:, None, :], (doms, cap, cap)
    ).reshape(doms * cap, cap)
    at_lane = lax.broadcasted_iota(jnp.int32, (doms * cap, cap), 1)
    at_slot = lax.broadcasted_iota(jnp.int32, (doms * cap, cap), 0) % cap
    route_column = jnp.sum(jnp.where(at_lane == at_slot, routes, 0.0), axis=1, keepdims=True)
    route_pick = (lane_row.astype(F32) == route_column).astype(F32).astype(BF16)
    loads[1].wait()
    hub_square = jnp.broadcast_to(hub_rows[...].astype(F32), (hub_count, hub_count))
    diagonal = lax.broadcasted_iota(jnp.int32, (hub_count, hub_count), 0) == (
        lax.broadcasted_iota(jnp.int32, (hub_count, hub_count), 1)
    )
    hub_column = jnp.sum(jnp.where(diagonal, hub_square, 0.0), axis=1, keepdims=True)
    hub_chosen = (lane_row.astype(F32) == hub_column).astype(F32)
    hub_pick = hub_chosen.astype(BF16)
    hub_spread = jnp.concatenate([hub_chosen] * groups, axis=0).T.astype(BF16)
    loads[2].wait()

    send_hubs[...] = dot(hub_pick, feats[...]).astype(BF16)
    pl.semaphore_wait(barrier, doms - 1 + groups - 1)
    hub_copies = share_to_groups(send_hubs, hubs_first)
    send_feats[...] = dot(route_pick, feats[...]).astype(BF16).reshape(send_feats.shape)
    feat_copies = to_doms(send_feats, slots_feats)
    loads[4].wait()
    grad_near = to_near(all_grad_out)
    slots_feats[dom] = send_feats[dom]
    hubs_first[group] = send_hubs[...]
    loads[3].wait()
    send_hist[...] = dot(route_pick, history[...]).astype(BF16).reshape(send_hist.shape)
    hist_copies = to_doms(send_hist, slots_hist)
    slots_hist[dom] = send_hist[dom]

    places = 3 * V_DEV
    place_of = lax.broadcasted_iota(jnp.int32, (places, V_DEV), 0)
    weights = jnp.zeros((V_DEV, places), F32)
    halo_tiles = HALO // TILE
    for load in loads[5:8]:
        load.wait()
    for tile in range(tile_vals.shape[1]):
        column = tile_cols[0:1, tile : tile + 1]
        target = jnp.where(column == 0, lane_row, lane_row + 2 * V_DEV)
        for halo in range(halo_tiles):
            slot = halo_index[halo * TILE : (halo + 1) * TILE].reshape(1, TILE) + V_DEV
            target = jnp.where(column == halo + 1, slot, target)
        chosen = (place_of == target).astype(F32).astype(BF16)
        weights = weights + dot(tile_vals[0, tile], chosen, (1, 1))
    own, slot, hub = (weights[:, n * V_DEV : (n + 1) * V_DEV] for n in range(3))
    own_pair, slot_pair, hub_pair = halves(own), halves(slot), halves(hub)

    loads[8].wait()
    agg_grad = dot(all_grad_out[dom], w_second_held[...], (1, 1)).astype(BF16)
    hub_terms[...] = apply_halves(halves(hub.T), agg_grad).astype(BF16).reshape(hub_terms.shape)
    term_copies = to_groups(hub_terms, hub_arrived)
    hub_arrived[group] = hub_terms[group]
    own_grad[...] = apply_halves(halves(own.T), agg_grad)

    first = apply_halves(own_pair, feats[...])
    arrived(feat_copies)
    first = first + apply_halves(slot_pair, slots_feats[...].reshape(V_DEV, D))
    arrived(hub_copies)
    first = first + apply_halves(hub_pair, hubs_first[...].reshape(V_DEV, D))
    agg_first = first.astype(BF16)
    all_agg[dom] = agg_first
    agg_near = to_near(all_agg)

    loads[9].wait()
    z_first = dot(agg_first, w_first_held[...])
    gate = 1.0 / (1.0 + jnp.exp(-z_first))
    fresh = (z_first * gate).astype(BF16)
    new_history[...] = fresh
    send_fresh[...] = dot(hub_pick, fresh).astype(BF16)
    fresh_copies = share_to_groups(send_fresh, hubs_second)
    hubs_second[group] = send_fresh[...]
    gate_slope[...] = gate * (1.0 + z_first * (1.0 - gate))

    arrived(term_copies)
    vertex_grad = own_grad[...] + dot(hub_spread, hub_arrived[...].reshape(V_DEV, D))
    embed_grad[...] = vertex_grad.astype(BF16)
    own_grad[...] = vertex_grad * gate_slope[...]
    for g in range(groups):
        for d in range(0, doms * share, TILE):
            start = g * doms * share + d
            block = own_grad[:, start : start + TILE].T.astype(BF16)
            for piece in range(TILE // share):
                dz_out[d // share + piece, g * share : (g + 1) * share, :] = block[
                    piece * share : (piece + 1) * share
                ]
    dz_copies = to_doms(dz_out, dz_in)
    dz_in[dom] = dz_out[dom]
    grad_parts, grad_passed = relay(grad_near, all_grad_out)

    arrived(hist_copies)
    second = apply_halves(own_pair, new_history[...])
    second = second + apply_halves(slot_pair, slots_hist[...].reshape(V_DEV, D))
    arrived(fresh_copies)
    second = second + apply_halves(hub_pair, hubs_second[...].reshape(V_DEV, D))
    wide = D // doms
    for d in range(doms):
        agg_out[d] = second[:, d * wide : (d + 1) * wide].T.astype(BF16)
    agg_copies = to_doms(agg_out, agg_in)
    agg_in[dom] = agg_out[dom]

    finish(grad_near, grad_parts, grad_passed, all_grad_out)
    arrived(agg_copies)
    blocks = jnp.concatenate([agg_in[d] for d in range(doms)], axis=1)
    total = dot(blocks, all_grad_out[...].reshape(doms * V_DEV, D))
    per_group = D // groups
    for g in range(groups):
        for n in range(0, per_group, TILE):
            start = g * per_group + n
            block = total[:, start : start + TILE].T
            second_terms[g, n : n + TILE, :] = block
            second_sent[g, n : n + TILE, :] = block.astype(BF16)
    second_copies = to_groups(second_sent, second_in)
    agg_parts, agg_passed = relay(agg_near, all_agg)

    finish(agg_near, agg_parts, agg_passed, all_agg)
    arrived(dz_copies)
    blocks = jnp.concatenate([dz_in[d] for d in range(doms)], axis=1)
    total = dot(blocks, all_agg[...].reshape(doms * V_DEV, D))
    first_terms[...] = total.reshape(first_terms.shape)
    first_sent[...] = total.astype(BF16).reshape(first_sent.shape)
    first_copies = to_groups(first_sent, first_in)

    arrived(second_copies)
    second_in[group] = jnp.zeros(second_in.shape[1:], BF16)
    total = second_terms[group]
    for g in range(groups):
        total = total + second_in[g].astype(F32)
    rows_out[...] = (total * factor).reshape(rows_out.shape)
    row_copies = to_doms(rows_out, rows_in)
    rows_in[dom] = rows_out[dom]

    arrived(first_copies)
    first_in[group] = jnp.zeros(first_in.shape[1:], BF16)
    total = first_terms[group]
    for g in range(groups):
        total = total + first_in[g].astype(F32)
    grad_first[...] = total * factor

    arrived(row_copies)
    for d in range(doms):
        grad_second[:, d * wide : (d + 1) * wide] = rows_in[d]
    for copy in used:
        copy.wait_send()


def write_kernel(*refs):
    given, written, staged, sems = refs[:4], refs[4:8], refs[8:12], refs[12]
    reads = [pltpu.make_async_copy(given[n], staged[n], sems.at[n]) for n in range(4)]
    writes = [pltpu.make_async_copy(staged[n], written[n], sems.at[n + 4]) for n in range(4)]
    for copy in reads:
        copy.start()
    for read, write in zip(reads, writes):
        read.wait()
        write.start()
    for copy in writes:
        copy.wait()


def in_kernel(
    feats, history, grad_out, w_first, w_second, send_index, halo_index, hub_rows, tile_cols, tile_vals
):
    groups, doms = lax.axis_size("group"), lax.axis_size("dom")
    share = D // (groups * doms)
    cap, hubs = send_index.shape[2], hub_rows.shape[1]
    wide, per_group = D // doms, D // groups
    copies = 5 * (doms - 1) + 5 * (groups - 1) + 16
    vmem = pl.BlockSpec(memory_space=pltpu.VMEM)
    hbm = pl.BlockSpec(memory_space=pltpu.HBM)
    held = pltpu.VMEM
    results = pl.pallas_call(
        functools.partial(window_kernel, groups, doms),
        out_shape=(
            jax.ShapeDtypeStruct((V_DEV, D), BF16),
            jax.ShapeDtypeStruct((V_DEV, D), BF16),
            jax.ShapeDtypeStruct((share, D), F32),
            jax.ShapeDtypeStruct((share, D), F32),
        ),
        in_specs=[hbm] * 10,
        out_specs=(vmem,) * 4,
        scratch_shapes=[
            held((D, D), BF16),
            held((D, D), BF16),
            held((V_DEV, D), BF16),
            held((V_DEV, D), BF16),
            held(send_index.shape, jnp.int32),
            held(halo_index.shape, jnp.int32),
            held(hub_rows.shape, jnp.int32),
            held(tile_cols.shape, jnp.int32),
            held(tile_vals.shape, BF16),
            held((doms, cap, D), BF16),
            held((doms, cap, D), BF16),
            held((hubs, D), BF16),
            held((hubs, D), BF16),
            held((doms, cap, D), BF16),
            held((doms, cap, D), BF16),
            held((groups, hubs, D), BF16),
            held((groups, hubs, D), BF16),
            held((doms, V_DEV, D), BF16),
            held((doms, V_DEV, D), BF16),
            held((groups, hubs, D), BF16),
            held((groups, hubs, D), BF16),
            held((V_DEV, D), F32),
            held((V_DEV, D), F32),
            held((doms, groups * share, V_DEV), BF16),
            held((doms, groups * share, V_DEV), BF16),
            held((doms, wide, V_DEV), BF16),
            held((doms, wide, V_DEV), BF16),
            held((groups, share, D), F32),
            held((groups, share, D), BF16),
            held((groups, share, D), BF16),
            held((groups, per_group, wide), F32),
            held((groups, per_group, wide), BF16),
            held((groups, per_group, wide), BF16),
            held((doms, share, wide), F32),
            held((doms, share, wide), F32),
            pltpu.SemaphoreType.DMA((10,)),
            pltpu.SemaphoreType.DMA((copies,)),
            pltpu.SemaphoreType.DMA((copies,)),
        ],
        compiler_params=pltpu.CompilerParams(
            collective_id=0, has_side_effects=True, vmem_limit_bytes=60 * 1024 * 1024
        ),
    )(
        feats,
        history,
        grad_out,
        w_first,
        w_second,
        send_index,
        halo_index,
        hub_rows,
        tile_cols,
        tile_vals,
    )
    shapes = [(part.shape, part.dtype) for part in results]
    return pl.pallas_call(
        write_kernel,
        out_shape=tuple(jax.ShapeDtypeStruct(*shape) for shape in shapes),
        in_specs=[pl.BlockSpec(memory_space=pl.ANY)] * 4,
        out_specs=(hbm,) * 4,
        scratch_shapes=[held(*shape) for shape in shapes] + [pltpu.SemaphoreType.DMA((8,))],
        compiler_params=pltpu.CompilerParams(vmem_limit_bytes=60 * 1024 * 1024),
    )(*results)


def fits_kernel(groups, doms, cap, hubs):
    return (
        D % (groups * doms * 16) == 0
        and TILE % (D // (groups * doms)) == 0
        and doms == 8
        and D // doms == V_DEV
        and doms * cap == V_DEV
        and groups * hubs == V_DEV
    )


def window(*args):
    send_index, hub_rows = args[5], args[7]
    groups, doms = lax.axis_size("group"), lax.axis_size("dom")
    if fits_kernel(groups, doms, send_index.shape[2], hub_rows.shape[1]):
        return in_kernel(*args)
    return on_device(*args)


def solution(mesh):
    placed = (
        P(("group", "dom"), None),
        P(("group", "dom"), None),
        P(("group", "dom"), None),
        P(),
        P(),
        P(("group", "dom"), None, None),
        P(("group", "dom")),
        P(("group", "dom"), None),
        P(("group", "dom"), None),
        P(("group", "dom"), None, None, None),
    )
    return jax.shard_map(
        window,
        mesh=mesh,
        in_specs=placed,
        out_specs=(
            P(("group", "dom"), None),
            P(("group", "dom"), None),
            P(("group", "dom"), None),
            P(("group", "dom"), None),
        ),
        check_vma=False,
    )
```
